32 devices in a mesh: rep: 16 (over z, x, core), dom: 2 (over y).
Axes of the slice: x: 2, y: 2, z: 4, core: 2. Of those that a mesh axis runs over, the one named last changes fastest.
Arguments:
- particle_locations: float32 [16, 3, 2048], P('rep', None, 'dom'), may hold values from 0 to 1.5
- particle_speeds: float32 [16, 3, 2048], P('rep', None, 'dom'), may hold values from -6 to 6
- current_pushes: float32 [16, 3, 2048], P('rep', None, 'dom'), may hold values from -6 to 6
- particle_kinds: int32 [16, 2048], P('rep', 'dom'), may hold values from 0 to 15
- halo_particle_labels: int32 [16, 1536], P('rep', 'dom'), may hold values from 0 to 1023
- adjacent_block_labels: int32 [16, 16, 4], P('rep', 'dom'), may hold values from 0 to 13
- adjacent_place_totals: int32 [16, 16], P('rep', 'dom'), may hold values from 1 to 4, as said below
- kind_vectors: bfloat16 [16, 128], replicated, may hold values from -6 to 6
- kind_inertia: float32 [16], replicated, may hold values from 1 to 4
- stepwise_distance_coefficients: float32 [2, 8, 128], replicated, may hold values from -2 to 2
- signal_scaling_factors: float32 [2, 128], replicated, may hold values from 0.1 to 1.9
- feature_blend_coefficients: bfloat16 [2, 128, 128], replicated, may hold values from -0.5 to 0.5
- target_projection_array: bfloat16 [128, 128], replicated, may hold values from -0.5 to 0.5
- source_projection_array: bfloat16 [128, 128], replicated, may hold values from -0.5 to 0.5
- push_distance_taper: float32 [8], replicated, may hold values from -4 to 4
- thermal_levels: float32 [16], replicated, may hold values from 0.5 to 2
- granted_swaps: int32 [16], replicated, may hold values from 0 to 15, as said below
Outputs:
- positions_out: float32 [16, 3, 2048], P('rep', None, 'dom')
- velocities_out: float32 [16, 3, 2048], P('rep', None, 'dom')
- forces_out: float32 [16, 3, 2048], P('rep', None, 'dom')
The draws below stay inside these ranges and needn't reach their ends.
Inputs may be any that keep to these rules, and one draw needn't show every extreme that they name: `halo_particle_labels`: each domain's block of 768 entries: the first 384 name its atoms imported by the next lower domain, the last 384 those imported by the next higher domain. `adjacent_block_labels`: numbers below 8 are the domain's own tiles; the rest are the imported atoms' tiles in extended order. `adjacent_place_totals`: in every replica some domain has all its tiles at 4 live slots. `granted_swaps`: each replica's partner is itself or a ladder neighbour, and the partner's partner is the replica. The pairs (0, 1), (7, 8) and (14, 15) are always accepted.
All inputs are finite; a program needn't handle non-finite values.
Results may differ from the reference program's by a relative error of at most 0.0067.
Values may be sent and summed in bfloat16 or wider, within the bound.
No kernel may reach another device: no remote copies, remote signals or barrier semaphores. Data moves between devices by JAX's collectives and lax.ppermute only.
A program may use at most 64 MiB of HBM per device.

```python
import math
import jax
import jax.numpy as jnp
from jax import lax

C = 128
NB = 8
SPECIES = 16
TILE = 128
NEI = 4
LAYERS = 2
ATOMS_DEV = 1024
GHOST = 384
TILES_DEV = 8
THERMAL_COPIES = 16
DOMAINS = 2
ATOMS = 2048


def draw_adjacent_place_totals(key, part):
    base_key, dense_key = jax.random.split(key)
    baseline = jax.random.randint(base_key, (THERMAL_COPIES, DOMAINS, TILES_DEV), 1, NEI + 1)
    crowded = jax.random.randint(dense_key, (THERMAL_COPIES, 1, 1), 0, DOMAINS)
    domain_ids = jnp.arange(DOMAINS, dtype=jnp.int32)[None, :, None]
    counts_all = jnp.where(domain_ids == crowded, NEI, baseline)
    return counts_all.reshape(THERMAL_COPIES, DOMAINS * TILES_DEV).astype(jnp.int32)


def draw_granted_swaps(key, part):
    accept_key = jax.random.fold_in(key, 7)
    replica_ids = jnp.arange(THERMAL_COPIES, dtype=jnp.int32)
    half_point = THERMAL_COPIES // 2
    accepted = jax.random.randint(accept_key, (THERMAL_COPIES,), 0, 2)
    forced = (replica_ids == 0) | (replica_ids == half_point - 1) | (replica_ids == THERMAL_COPIES - 2)
    even_free = (replica_ids % 2 == 0) & (replica_ids >= 2) & (replica_ids <= THERMAL_COPIES - 4) & (replica_ids != half_point - 2) & (replica_ids != half_point)
    is_low = forced | even_free & (accepted == 1)
    below_low = jnp.concatenate([jnp.zeros((1,), dtype=bool), is_low[:-1]])
    partner_ids = jnp.where(is_low, replica_ids + 1, jnp.where(below_low, replica_ids - 1, replica_ids))
    return partner_ids.astype(jnp.int32)


def set_ends(values, stream_key, low, largest):
    place = [jax.random.randint(jax.random.fold_in(stream_key, axis), (), 0, length) for axis, length in enumerate(values.shape)]
    widest = values.shape.index(max(values.shape))
    beside = place[:widest] + [(place[widest] + 1) % values.shape[widest]] + place[widest + 1:]
    return values.at[tuple(place)].set(low).at[tuple(beside)].set(largest)


def shard_levels(own_key, shape, shards, smallest, largest):
    factor_of, own = 1.0, jax.random.fold_in(own_key, 6)
    for axis_at, blocks in shards:
        draws = jnp.exp(jax.random.uniform(jax.random.fold_in(own, axis_at), (blocks,), jnp.float32, smallest / len(shards), largest / len(shards)))
        factor_of = factor_of * jnp.repeat(draws, shape[axis_at] // blocks).reshape([-1 if axis == axis_at else 1 for axis in range(len(shape))])
    return factor_of


def normal_values(stream_key, dims, deviation, limit, shards=(), kind=jnp.bfloat16):
    values = deviation * jax.random.normal(stream_key, dims, jnp.float32)
    if shards:
        values = values * shard_levels(stream_key, dims, shards, -0.22, 0.18)
    return jnp.clip(values, -limit, limit).astype(kind)


def setup_inputs(seed: int = 0) -> dict:
    key_of = jax.random.split(jax.random.key(seed), 18)
    return {
        "particle_locations": jnp.clip(1.5 * jax.random.uniform(key_of[0], (THERMAL_COPIES, 3, ATOMS), jnp.float32) ** shard_levels(key_of[0], (THERMAL_COPIES, 3, ATOMS), ((0, 16), (2, 2)), -0.2, 0.2), 0.0, 1.5),
        "particle_speeds": normal_values(key_of[1], (THERMAL_COPIES, 3, ATOMS), 1.0, 6.0, ((0, 16), (2, 2)), jnp.float32),
        "current_pushes": normal_values(key_of[2], (THERMAL_COPIES, 3, ATOMS), 1.0, 6.0, ((0, 16), (2, 2)), jnp.float32),
        "particle_kinds": set_ends(jax.random.randint(key_of[3], (THERMAL_COPIES, ATOMS), 0, SPECIES), jax.random.fold_in(key_of[3], 1), 0, SPECIES - 1).astype(jnp.int32),
        "halo_particle_labels": set_ends(jax.random.randint(key_of[4], (THERMAL_COPIES, 2 * GHOST * DOMAINS), 0, ATOMS_DEV), jax.random.fold_in(key_of[4], 1), 0, ATOMS_DEV - 1).astype(jnp.int32),
        "adjacent_block_labels": set_ends(jax.random.randint(key_of[5], (THERMAL_COPIES, TILES_DEV * DOMAINS, NEI), 0, 7 * TILES_DEV // 4), jax.random.fold_in(key_of[5], 1), 0, (7 * TILES_DEV // 4) - 1).astype(jnp.int32),
        "adjacent_place_totals": draw_adjacent_place_totals(jax.random.fold_in(key_of[17], 71), 0),
        "kind_vectors": normal_values(key_of[7], (SPECIES, C), 1.0, 6.0),
        "kind_inertia": jnp.clip(jnp.exp(jax.random.uniform(key_of[8], (SPECIES,), jnp.float32, math.log(1.0), math.log(4.0))), 1.0, 4.0),
        "stepwise_distance_coefficients": normal_values(key_of[9], (LAYERS, NB, C), NB ** -0.5, 2.0, (), jnp.float32),
        "signal_scaling_factors": jnp.clip(1.0 + 0.18 * jax.random.normal(key_of[10], (LAYERS, C), jnp.float32), 0.1, 1.9),
        "feature_blend_coefficients": normal_values(key_of[11], (LAYERS, C, C), C ** -0.5, 0.5),
        "target_projection_array": normal_values(key_of[12], (C, C), C ** -0.5, 0.5),
        "source_projection_array": normal_values(key_of[13], (C, C), C ** -0.5, 0.5),
        "push_distance_taper": normal_values(key_of[14], (NB,), 1.0, 4.0, (), jnp.float32),
        "thermal_levels": jnp.clip(jnp.exp(jax.random.uniform(key_of[15], (THERMAL_COPIES,), jnp.float32, math.log(0.5), math.log(2.0))), 0.5, 2.0),
        "granted_swaps": draw_granted_swaps(jax.random.fold_in(key_of[17], 71), 0),
    }


slab_width = 1.5
time_step = 0.5
basis_width = 0.3
norm_eps = 1e-06

def pair_basis(near_pos, far_pos, live_flag):
    offsets = far_pos[:, None, :] - near_pos[:, :, None]
    distance = jnp.sqrt(lax.optimization_barrier(jnp.sum(offsets * offsets, axis=0)))
    centers = basis_width * jnp.arange(NB, dtype=jnp.float32)
    scaled = (distance[None, :, :] - centers[:, None, None]) / basis_width
    return (jnp.exp(-scaled * scaled) * live_flag).astype(jnp.bfloat16)

def species_onehot(labels, width):
    return labels[:, None] == jnp.arange(width, dtype=jnp.int32)[None, :]

def embed_rows(labels, kind_vectors):
    onehot = species_onehot(labels, kind_vectors.shape[0]).astype(jnp.bfloat16)
    return jnp.dot(onehot, kind_vectors, preferred_element_type=jnp.float32).astype(jnp.bfloat16)

def tile_messages(ext_pos, ext_hidden, tile_lists, live_counts, radial_row):

    def one_tile(tile_index):
        near_pos = lax.dynamic_slice_in_dim(ext_pos, tile_index * TILE, TILE, 1)
        summed = jnp.zeros((NB, TILE, ext_hidden.shape[1]), jnp.float32)
        for slot_index in range(NEI):
            source = tile_lists[tile_index, slot_index].astype(jnp.int32)
            far_pos = lax.dynamic_slice_in_dim(ext_pos, source * TILE, TILE, 1)
            far_feat = lax.dynamic_slice_in_dim(ext_hidden, source * TILE, TILE, 0)
            live_flag = (slot_index < live_counts[tile_index]).astype(jnp.float32)
            basis_val = pair_basis(near_pos, far_pos, live_flag)
            summed = summed + jnp.einsum('bij,jc->bic', basis_val.astype(jnp.float32), far_feat.astype(jnp.float32), precision=lax.Precision.HIGHEST)
        return jnp.einsum('bic,bc->ic', summed, radial_row, precision=lax.Precision.HIGHEST)
    tile_total = tile_lists.shape[0]
    result = lax.map(one_tile, jnp.arange(tile_total, dtype=jnp.int32))
    return result.reshape(tile_total * TILE, -1)

def refresh(hidden, messages, gain_row, mix_matrix):
    inverse = lax.rsqrt(lax.optimization_barrier(jnp.mean(messages * messages, axis=-1, keepdims=True)) + norm_eps)
    activation = jax.nn.silu(messages * inverse * gain_row).astype(jnp.bfloat16)
    return (hidden.astype(jnp.float32) + jnp.dot(activation, mix_matrix, preferred_element_type=jnp.float32)).astype(jnp.bfloat16)

def tile_forces(ext_pos, query, ext_keys, tile_lists, live_counts, push_distance_taper):
    factor = 1.0 / math.sqrt(query.shape[1] * NEI * TILE)

    def one_tile(tile_index):
        near_pos = lax.dynamic_slice_in_dim(ext_pos, tile_index * TILE, TILE, 1)
        asking = lax.dynamic_slice_in_dim(query, tile_index * TILE, TILE, 0)
        summed = jnp.zeros((3, TILE), jnp.float32)
        for slot_index in range(NEI):
            source = tile_lists[tile_index, slot_index].astype(jnp.int32)
            far_pos = lax.dynamic_slice_in_dim(ext_pos, source * TILE, TILE, 1)
            far_keys = lax.dynamic_slice_in_dim(ext_keys, source * TILE, TILE, 0)
            live_flag = (slot_index < live_counts[tile_index]).astype(jnp.float32)
            basis_val = pair_basis(near_pos, far_pos, live_flag)
            envelope = jnp.einsum('bij,b->ij', basis_val.astype(jnp.float32), push_distance_taper, precision=lax.Precision.HIGHEST)
            scores = jnp.einsum('ic,jc->ij', asking.astype(jnp.float32), far_keys.astype(jnp.float32), precision=lax.Precision.HIGHEST)
            pair_weight = scores * envelope * factor
            summed = summed + jnp.einsum('dj,ij->di', far_pos, pair_weight, precision=lax.Precision.HIGHEST) - near_pos * lax.optimization_barrier(jnp.sum(pair_weight, axis=1))[None, :]
        return summed
    result = lax.map(one_tile, jnp.arange(tile_lists.shape[0], dtype=jnp.int32))
    return jnp.transpose(result, (1, 0, 2)).reshape(3, -1)

def attach(stacked, ghosts, axis_pos):
    packs = jax.vmap(lambda domain_block, domain_rows: jnp.take(domain_block, domain_rows, axis=axis_pos))(stacked, ghosts)
    ghost_count = ghosts.shape[1] // 2
    from_lower = lax.slice_in_dim(jnp.roll(packs, 1, axis=0), ghost_count, 2 * ghost_count, axis=axis_pos + 1)
    from_upper = lax.slice_in_dim(jnp.roll(packs, -1, axis=0), 0, ghost_count, axis=axis_pos + 1)
    return (from_lower, from_upper)

def extend_rows(stacked, ghosts):
    from_lower, from_upper = attach(stacked, ghosts, 0)
    return jnp.concatenate([stacked, from_lower, from_upper], axis=1)

def replica_step(coords, speeds, old_force, labels, ghost_rows, tile_rows, count_rows, weights):
    kind_vectors, kind_inertia, stepwise_distance_coefficients, signal_scaling_factors, feature_blend_coefficients, target_projection_array, source_projection_array, push_distance_taper = weights
    chosen_mass = jnp.where(species_onehot(labels, kind_inertia.shape[0]), kind_inertia[None, :], 0.0)
    inv_mass = 1.0 / lax.optimization_barrier(jnp.sum(chosen_mass, axis=1))
    displaced = coords + time_step * speeds + 0.5 * time_step * time_step * old_force * inv_mass[None, :]
    half_speed = speeds + 0.5 * time_step * old_force * inv_mass[None, :]
    ghosts = ghost_rows.reshape(DOMAINS, 2 * GHOST)
    tile_lists = tile_rows.reshape(DOMAINS, TILES_DEV, NEI)
    live_counts = count_rows.reshape(DOMAINS, TILES_DEV)
    domain_pos = jnp.transpose(displaced.reshape(3, DOMAINS, ATOMS_DEV), (1, 0, 2))
    shift_vec = slab_width * (jnp.arange(3, dtype=jnp.int32) == 0).astype(jnp.float32)[:, None]
    from_lower, from_upper = attach(domain_pos, ghosts, 1)
    ext_pos = jnp.concatenate([domain_pos, from_lower - shift_vec, from_upper + shift_vec], axis=2)
    hidden = embed_rows(labels, kind_vectors).reshape(DOMAINS, ATOMS_DEV, -1)
    for layer_step in range(LAYERS):
        ext_hidden = extend_rows(hidden, ghosts)
        radial_row = stepwise_distance_coefficients[layer_step]
        messages = lax.map(lambda items: tile_messages(items[0], items[1], items[2], items[3], radial_row), (ext_pos, ext_hidden, tile_lists, live_counts))
        hidden = refresh(hidden, messages, signal_scaling_factors[layer_step], feature_blend_coefficients[layer_step])
    query = jnp.dot(hidden, target_projection_array, preferred_element_type=jnp.float32).astype(jnp.bfloat16)
    keys_local = jnp.dot(hidden, source_projection_array, preferred_element_type=jnp.float32).astype(jnp.bfloat16)
    ext_keys = extend_rows(keys_local, ghosts)
    forces = lax.map(lambda items: tile_forces(items[0], items[1], items[2], items[3], items[4], push_distance_taper), (ext_pos, query, ext_keys, tile_lists, live_counts))
    updated_push = jnp.transpose(forces, (1, 0, 2)).reshape(3, ATOMS)
    updated_velocity = half_speed + 0.5 * time_step * updated_push * inv_mass[None, :]
    return (displaced, updated_velocity, updated_push)

def reference(particle_locations, particle_speeds, current_pushes, particle_kinds, halo_particle_labels, adjacent_block_labels, adjacent_place_totals, kind_vectors, kind_inertia, stepwise_distance_coefficients, signal_scaling_factors, feature_blend_coefficients, target_projection_array, source_projection_array, push_distance_taper, thermal_levels, granted_swaps):
    weights = (kind_vectors, kind_inertia, stepwise_distance_coefficients, signal_scaling_factors, feature_blend_coefficients, target_projection_array, source_projection_array, push_distance_taper)

    def per_replica(items):
        return replica_step(items[0], items[1], items[2], items[3], items[4], items[5], items[6], weights)
    displaced, updated_velocity, updated_push = lax.map(per_replica, (particle_locations, particle_speeds, current_pushes, particle_kinds, halo_particle_labels, adjacent_block_labels, adjacent_place_totals))
    thermal_quotient = jnp.sqrt(thermal_levels / thermal_levels[granted_swaps])
    return (displaced[granted_swaps], updated_velocity[granted_swaps] * thermal_quotient[:, None, None], updated_push[granted_swaps])
```

```python
import functools
import math

import jax
import jax.numpy as jnp
from jax import lax
from jax.experimental import pallas as pl
from jax.experimental.pallas import tpu as pltpu
from jax.sharding import PartitionSpec as P

NB = 8
TILE = 128
NEI = 4

slab_width = 1.5
time_step = 0.5
basis_width = 0.3
norm_eps = 1e-06

f32 = jnp.float32
bf16 = jnp.bfloat16

LOG2E = math.log2(math.e)
SCALE = math.sqrt(LOG2E) / basis_width
LIFT = 24.0
FAR = LOG2E * 400.0


def distinct(offsets, count):
    return list(dict.fromkeys(o % count for o in offsets))


def domain_sets(count):
    layer1 = distinct([0, -1, 1], count)
    layer0 = distinct(layer1 + [o + s for o in layer1 for s in (-1, 1)], count)
    held = distinct(layer0 + [o + s for o in layer0 for s in (-1, 1)], count)
    return layer1, layer0, held


def dot(a, b):
    return jnp.dot(a, b, preferred_element_type=f32)


def pack_kernel(loc, speed, push, kinds, ghosts, lists, counts, inertia, out):
    labels = kinds[...]
    mass = jnp.zeros(labels.shape, f32)
    for s in range(inertia.shape[0]):
        mass = jnp.where(labels == s, inertia[s], mass)
    inv_mass = 1.0 / mass
    atoms, tiles = labels.shape[1], counts.shape[1]
    out[...] = jnp.zeros(out.shape, f32)
    for d in range(3):
        out[d : d + 1, 0:atoms] = (
            loc[d] + time_step * speed[d] + 0.5 * time_step * time_step * push[d] * inv_mass
        )
        out[3 + d : 4 + d, 0:atoms] = speed[d] + 0.5 * time_step * push[d] * inv_mass
    out[6:7, 0:atoms] = labels.astype(f32)
    out[7:8, 0 : ghosts.shape[1]] = ghosts[...].astype(f32)
    out[0:NEI, atoms : atoms + tiles] = lists[0].astype(f32)
    out[NEI : NEI + 1, atoms : atoms + tiles] = counts[...].astype(f32)


def weights_kernel(kind, coef, gain, mix, target, u_parts, kind_t, w_cols, gain_cols, mix_t, target_t):
    kinds_f = jnp.transpose(kind[...].astype(f32), (1, 0))
    kind_t[...] = kinds_f.astype(bf16)
    coef_t = [jnp.transpose(coef[layer], (1, 0)) for layer in range(2)]
    columns = []
    for b in range(NB):
        columns.append(kinds_f * (coef_t[0][:, b : b + 1] * math.exp(-b * b)))
        w_cols[b] = jnp.broadcast_to(coef_t[1][:, b : b + 1] * math.exp(-b * b), (TILE, TILE))
    u = jnp.concatenate(columns, axis=1)
    high = u.astype(bf16)
    u_parts[...] = jnp.concatenate([high, (u - high.astype(f32)).astype(bf16), high], axis=1)
    gain_t = jnp.transpose(gain[...], (1, 0))
    for layer in range(2):
        gain_cols[layer] = jnp.broadcast_to(gain_t[:, layer : layer + 1], (TILE, TILE))
        mix_t[layer] = jnp.transpose(mix[layer].astype(f32), (1, 0)).astype(bf16)
    target_t[...] = jnp.transpose(target[...].astype(f32), (1, 0)).astype(bf16)


def lanes_of(parts):
    return jnp.concatenate(parts, axis=1)


def refresh(hidden, messages, gain, mix_t):
    activations = []
    for block in messages:
        block = block * math.exp(-LIFT)
        inverse = lax.rsqrt(jnp.mean(block * block, axis=0, keepdims=True) + norm_eps)
        v = block * inverse * gain
        activations.append((v / (1.0 + jnp.exp(-v))).astype(bf16))
    mixed = dot(mix_t, lanes_of(activations))
    return [
        (block + mixed[:, t * TILE : (t + 1) * TILE]).astype(bf16)
        for t, block in enumerate(hidden)
    ]


def main_kernel(plan, *refs):
    count, atoms, ghost = plan
    layer1, layer0, held = domain_sets(count)
    tiles = atoms // TILE
    ghost_tiles = ghost // TILE
    ext_tiles = tiles + 2 * ghost_tiles
    n = len(held)
    me, swaps, levels, inertia, taper = refs[:5]
    data = dict(zip(held, refs[5 : 5 + n]))
    u_parts, kind_t, w_cols, gain_cols, mix_t, target_t, source = refs[5 + n : 12 + n]
    pos_out, vel_out, force_out = refs[12 + n : 15 + n]
    (
        basis,
        far_t,
        near_rhs,
        onehot,
        split_pos,
        diffs,
        species_sums,
        ghost_pick,
        hidden1,
        hidden2,
        ext_hidden,
        message_rows,
        turned,
        asked,
        pulls,
        ints,
        sm,
        sem,
    ) = refs[15 + n :]
    kept = basis.shape[0]

    for at, o in enumerate(layer0):
        ints[at] = data[o][:, atoms : atoms + TILE].astype(jnp.int32)
    copies = [
        pltpu.make_async_copy(ints.at[at], sm.at[at], sem.at[at]) for at in range(len(layer0))
    ]
    for c in copies:
        c.start()

    row_id = lax.broadcasted_iota(jnp.int32, (8, TILE), 0)
    species_id = lax.broadcasted_iota(jnp.int32, (16, TILE), 0).astype(f32)
    ones_block = jnp.where(row_id < 3, 1.0, 0.0)

    def picked(o, first):
        src = data[o]
        idx = src[7:8, first : first + TILE].astype(jnp.int32)
        idx = jnp.broadcast_to(idx, (8, TILE))
        lane = idx & (TILE - 1)
        block = idx // TILE
        got = jnp.zeros((8, TILE), f32)
        for c in range(tiles):
            here = jnp.take_along_axis(
                src[:, c * TILE : (c + 1) * TILE], lane, axis=1, mode="promise_in_bounds"
            )
            got = jnp.where(block == c, here, got)
        return got

    wide_row = lax.broadcasted_iota(jnp.int32, (24, 3 * TILE), 0)
    wide_block = lax.broadcasted_iota(jnp.int32, (24, 3 * TILE), 1) // TILE
    selector = jnp.where((wide_row & 7) == wide_block, 1.0, 0.0)

    for at, o in enumerate(layer0):
        lower, upper = (o - 1) % count, (o + 1) % count
        for e in range(ext_tiles):
            if e < tiles:
                block, shift = data[o][:, e * TILE : (e + 1) * TILE], 0.0
            elif e < tiles + ghost_tiles:
                block, shift = picked(lower, ghost + (e - tiles) * TILE), -slab_width
            else:
                block, shift = picked(upper, (e - tiles - ghost_tiles) * TILE), slab_width
            moved = jnp.where(row_id == 0, block + shift, block) * SCALE
            moved = jnp.where(row_id < 3, moved, jnp.where(row_id == 3, 1.0, 0.0))
            onehot[at, e] = jnp.where(species_id == block[6:7, :], 1.0, 0.0).astype(bf16)
            hi = moved.astype(bf16).astype(f32)
            mid = (moved - hi).astype(bf16).astype(f32)
            low = moved - hi - mid
            stack = jnp.concatenate([hi, mid, low, ones_block], axis=0)
            far_t[at, e] = jnp.transpose(stack, (1, 0)).astype(bf16)
            if o == 0:
                split_pos[e] = stack.astype(bf16)
            if e < tiles:
                less = lanes_of(
                    [
                        jnp.where(
                            row_id == 0,
                            -hi[d : d + 1],
                            jnp.where(
                                row_id == 1,
                                -mid[d : d + 1],
                                jnp.where(row_id == 2, -low[d : d + 1], 0.0),
                            ),
                        )
                        for d in range(3)
                    ]
                )
                near_rhs[at, e] = jnp.concatenate([selector, less], axis=0).astype(bf16)

    for c in copies:
        c.wait()

    def offsets(at, t):
        far = jnp.concatenate([far_t[at, sm[at, k, t]] for k in range(NEI)], axis=0)
        return dot(far, near_rhs[at, t])

    def species_step(at, t):
        lhs = lanes_of([onehot[at, sm[at, k, t]] for k in range(NEI)])
        sums = dot(lhs, basis[jnp.minimum(at, kept - 1), t])
        sums = jnp.concatenate([sums[:, b * TILE : (b + 1) * TILE] for b in range(NB)], axis=0)
        high = sums.astype(bf16)
        low = (sums - high.astype(f32)).astype(bf16)
        return jnp.concatenate([high, high, low], axis=0)

    steps = len(layer0) * tiles
    diffs[...] = offsets(0, 0)

    def basis_step(s, _):
        before = jnp.maximum(s - 1, 0)
        after = jnp.minimum(s + 1, steps - 1)
        at, t = s // tiles, s % tiles
        species_sums[before // tiles, before % tiles] = species_step(before // tiles, before % tiles)
        upcoming = offsets(after // tiles, after % tiles)
        place = jnp.minimum(at, kept - 1)
        for k in range(NEI):
            top = jnp.where(k < sm[at, NEI, t], f32(LIFT * LOG2E), f32(-1e30))
            rows = slice(k * TILE, (k + 1) * TILE)
            square = None
            for d in range(3):
                off = diffs[rows, d * TILE : (d + 1) * TILE]
                square = off * off if square is None else square + off * off
            square = jnp.minimum(jnp.maximum(square, 1e-30), FAR)
            length = square * lax.rsqrt(square)
            step = (4.0 * math.sqrt(LOG2E)) * length
            ratio = jnp.exp2((2.0 * math.sqrt(LOG2E)) * length)
            power = top - square
            for b in range(0, NB, 2):
                value = jnp.exp2(power)
                basis[place, t, rows, b * TILE : (b + 1) * TILE] = value.astype(bf16)
                basis[place, t, rows, (b + 1) * TILE : (b + 2) * TILE] = (value * ratio).astype(bf16)
                power = power + step
        diffs[...] = upcoming
        return 0

    lax.fori_loop(0, steps, basis_step, 0)
    species_sums[len(layer0) - 1, tiles - 1] = species_step(len(layer0) - 1, tiles - 1)

    for at, o in enumerate(layer0):
        chosen = data[o][7:8, 0 : 2 * ghost]

        def pick_step(c, _):
            first = pl.multiple_of(c * TILE, TILE)
            rows = lax.broadcasted_iota(jnp.int32, (TILE, 2 * ghost), 0) + first
            ghost_pick[at, pl.ds(first, TILE), :] = jnp.where(
                rows.astype(f32) == chosen, 1.0, 0.0
            ).astype(bf16)
            return 0

        lax.fori_loop(0, tiles, pick_step, 0)

    for at in range(len(layer0)):
        messages = dot(u_parts[...], lanes_of([species_sums[at, t] for t in range(tiles)]))
        hidden0 = dot(kind_t[...], lanes_of([onehot[at, t] for t in range(tiles)]))
        split = lambda x: [x[:, t * TILE : (t + 1) * TILE] for t in range(tiles)]
        for t, block in enumerate(
            refresh(split(hidden0), split(messages), gain_cols[0], mix_t[0])
        ):
            hidden1[at, t] = block

    def extend(source_hidden, sets, o):
        for t in range(tiles):
            ext_hidden[t] = source_hidden[sets.index(o), t]
        for side, other in ((0, (o - 1) % count), (1, (o + 1) % count)):
            at = sets.index(other)
            rows = lanes_of([source_hidden[at, t] for t in range(tiles)])
            first = ghost if side == 0 else 0
            got = dot(
                rows, ghost_pick[layer0.index(other), :, first : first + ghost]
            ).astype(bf16)
            for g in range(ghost_tiles):
                ext_hidden[tiles + side * ghost_tiles + g] = got[:, g * TILE : (g + 1) * TILE]

    for keep, o in enumerate(layer1):
        at = layer0.index(o)
        extend(hidden1, layer0, o)

        def second_step(t, _):
            lhs = lanes_of([ext_hidden[sm[at, k, t]] for k in range(NEI)])
            sums = dot(lhs, basis[keep, t])
            messages = jnp.zeros((TILE, TILE), f32)
            for b in range(NB):
                messages = messages + sums[:, b * TILE : (b + 1) * TILE] * w_cols[b]
            message_rows[t] = messages
            return 0

        lax.fori_loop(0, tiles, second_step, 0, unroll=2)
        for t, block in enumerate(
            refresh(
                [hidden1[at, t].astype(f32) for t in range(tiles)],
                [message_rows[t] for t in range(tiles)],
                gain_cols[1],
                mix_t[1],
            )
        ):
            hidden2[keep, t] = block

    extend(hidden2, layer1, 0)
    for e in range(ext_tiles):
        turned[e] = jnp.transpose(ext_hidden[e].astype(f32), (1, 0)).astype(bf16)
    query = dot(target_t[...], lanes_of([ext_hidden[t] for t in range(tiles)])).astype(bf16)
    wanted = dot(source[...], query).astype(bf16)
    for t in range(tiles):
        asked[t] = wanted[:, t * TILE : (t + 1) * TILE]

    factor = math.exp(-LIFT) / math.sqrt(TILE * NEI * TILE) / SCALE

    def force_step(t, _):
        lhs = jnp.concatenate([turned[sm[0, k, t]] for k in range(NEI)], axis=0)
        scores = dot(lhs, asked[t])
        envelope = jnp.zeros((NEI * TILE, TILE), f32)
        for b in range(NB):
            envelope = envelope + basis[0, t, :, b * TILE : (b + 1) * TILE].astype(f32) * (
                taper[b] * (math.exp(-b * b) * factor)
            )
        weight = (scores * envelope).astype(bf16)
        places = lanes_of([split_pos[sm[0, k, t]] for k in range(NEI)])
        got = dot(places, weight)
        pulls[t] = got[0:8] + got[8:16] + got[16:24]
        return 0

    lax.fori_loop(0, tiles, force_step, 0, unroll=2)

    p = swaps[me[0]]
    quotient = jnp.sqrt(jnp.full((1, TILE), levels[me[0]], f32) / jnp.full((1, TILE), levels[p], f32))
    own = data[0]
    labels = own[6:7, 0:atoms]
    mass = jnp.zeros(labels.shape, f32)
    for s in range(inertia.shape[0]):
        mass = jnp.where(labels == s, inertia[s], mass)
    inv_mass = 1.0 / mass
    for t in range(tiles):
        lanes = slice(t * TILE, (t + 1) * TILE)
        got = pulls[t]
        force = got - own[:, lanes] * SCALE * got[3:4]
        velocity = own[3:6, lanes] + 0.5 * time_step * force[0:3] * inv_mass[:, lanes]
        velocity = velocity * quotient
        for d in range(3):
            pos_out[d, :, lanes] = own[d : d + 1, lanes]
            force_out[d, :, lanes] = force[d : d + 1]
            vel_out[d, :, lanes] = velocity[d : d + 1]


def local(
    count,
    replicas,
    particle_locations,
    particle_speeds,
    current_pushes,
    particle_kinds,
    halo_particle_labels,
    adjacent_block_labels,
    adjacent_place_totals,
    kind_vectors,
    kind_inertia,
    stepwise_distance_coefficients,
    signal_scaling_factors,
    feature_blend_coefficients,
    target_projection_array,
    source_projection_array,
    push_distance_taper,
    thermal_levels,
    granted_swaps,
):
    atoms = particle_locations.shape[2]
    ghost = halo_particle_labels.shape[1] // 2
    channels = kind_vectors.shape[1]
    tiles = atoms // TILE
    ext_tiles = tiles + 2 * (ghost // TILE)
    layer1, layer0, held = domain_sets(count)
    vmem = pl.BlockSpec(memory_space=pltpu.VMEM)
    smem = pl.BlockSpec(memory_space=pltpu.SMEM)
    shape = jax.ShapeDtypeStruct

    packed = pl.pallas_call(
        pack_kernel,
        out_shape=shape((8, atoms + TILE), f32),
        in_specs=[vmem] * 7 + [smem],
        out_specs=vmem,
    )(
        jnp.transpose(particle_locations, (1, 0, 2)),
        jnp.transpose(particle_speeds, (1, 0, 2)),
        jnp.transpose(current_pushes, (1, 0, 2)),
        particle_kinds,
        halo_particle_labels,
        jnp.transpose(adjacent_block_labels, (0, 2, 1)),
        adjacent_place_totals,
        kind_inertia,
    )

    me = lax.axis_index("rep")
    partner = granted_swaps[me]
    even = [(i, i ^ 1) for i in range(replicas)]
    odd = [(i, ((i + 1) ^ 1) - 1) for i in range(1, replicas - 1)]
    odd_all = [(a * count + d, b * count + d) for a, b in odd for d in range(count)] + [
        (r * count + d, r * count + (d + 1) % count) for r in (0, replicas - 1) for d in range(count)
    ]
    from_even = lax.ppermute(packed, "rep", even)
    from_odd = lax.ppermute(packed, ("rep", "dom"), odd_all)
    low = jnp.minimum(me, partner)
    chosen = jnp.where(partner == me, packed, jnp.where(low % 2 == 0, from_even, from_odd))
    data = [
        chosen
        if o == 0
        else lax.ppermute(chosen, "dom", [((d + o) % count, d) for d in range(count)])
        for o in held
    ]

    weights = pl.pallas_call(
        weights_kernel,
        out_shape=[
            shape((channels, 3 * NB * kind_vectors.shape[0]), bf16),
            shape((channels, kind_vectors.shape[0]), bf16),
            shape((NB, channels, TILE), f32),
            shape((2, channels, TILE), f32),
            shape((2, channels, channels), bf16),
            shape((channels, channels), bf16),
        ],
        in_specs=[vmem] * 5,
        out_specs=[vmem] * 6,
        cost_estimate=pl.CostEstimate(flops=10**6, bytes_accessed=10**6, transcendentals=0),
    )(
        kind_vectors,
        stepwise_distance_coefficients,
        signal_scaling_factors,
        feature_blend_coefficients,
        target_projection_array,
    )

    outs = pl.pallas_call(
        functools.partial(main_kernel, (count, atoms, ghost)),
        out_shape=[shape((3, 1, atoms), f32)] * 3,
        in_specs=[smem] * 5 + [vmem] * (len(held) + 7),
        out_specs=[vmem] * 3,
        scratch_shapes=[
            pltpu.VMEM((len(layer1) + (len(layer0) > len(layer1)), tiles, NEI * TILE, NB * TILE), bf16),
            pltpu.VMEM((len(layer0), ext_tiles, TILE, 32), bf16),
            pltpu.VMEM((len(layer0), tiles, 32, 3 * TILE), bf16),
            pltpu.VMEM((len(layer0), ext_tiles, 16, TILE), bf16),
            pltpu.VMEM((ext_tiles, 32, TILE), bf16),
            pltpu.VMEM((NEI * TILE, 3 * TILE), f32),
            pltpu.VMEM((len(layer0), tiles, 3 * NB * 16, TILE), bf16),
            pltpu.VMEM((len(layer0), atoms, 2 * ghost), bf16),
            pltpu.VMEM((len(layer0), tiles, TILE, TILE), bf16),
            pltpu.VMEM((len(layer1), tiles, TILE, TILE), bf16),
            pltpu.VMEM((ext_tiles, TILE, TILE), bf16),
            pltpu.VMEM((tiles, TILE, TILE), f32),
            pltpu.VMEM((ext_tiles, TILE, TILE), bf16),
            pltpu.VMEM((tiles, TILE, TILE), bf16),
            pltpu.VMEM((tiles, 8, TILE), f32),
            pltpu.VMEM((len(layer0), 8, TILE), jnp.int32),
            pltpu.SMEM((len(layer0), 8, TILE), jnp.int32),
            pltpu.SemaphoreType.DMA((len(layer0),)),
        ],
        compiler_params=pltpu.CompilerParams(vmem_limit_bytes=58 * 2**20),
    )(
        me.reshape(1),
        granted_swaps,
        thermal_levels,
        kind_inertia,
        push_distance_taper,
        *data,
        *weights,
        source_projection_array,
    )
    return tuple(jnp.transpose(x, (1, 0, 2)) for x in outs)


def solution(mesh):
    in_specs = (
        P("rep", None, "dom"),
        P("rep", None, "dom"),
        P("rep", None, "dom"),
        P("rep", "dom"),
        P("rep", "dom"),
        P("rep", "dom", None),
        P("rep", "dom"),
    ) + (P(),) * 10
    out_specs = (P("rep", None, "dom"), P("rep", None, "dom"), P("rep", None, "dom"))
    step = functools.partial(local, mesh.shape["dom"], mesh.shape["rep"])
    return jax.shard_map(step, mesh=mesh, in_specs=in_specs, out_specs=out_specs, check_vma=False)
```

```python
import functools
import math

import jax
import jax.numpy as jnp
from jax import lax
from jax.experimental import pallas as pl
from jax.experimental.pallas import tpu as pltpu
from jax.sharding import PartitionSpec as P

NB = 8
TILE = 128
NEI = 4

slab_width = 1.5
time_step = 0.5
basis_width = 0.3
norm_eps = 1e-06

f32 = jnp.float32
bf16 = jnp.bfloat16

LOG2E = math.log2(math.e)
SCALE = math.sqrt(LOG2E) / basis_width
TOP = 34.0
UNLIFT = 2.0**-TOP
STEEP = 4.0 * LOG2E
FAR = (40.0 * LOG2E) ** 2
BODY = 4


def distinct(offsets, count):
    return list(dict.fromkeys(o % count for o in offsets))


def domain_sets(count):
    layer1 = distinct([0, -1, 1], count)
    layer0 = distinct(layer1 + [o + s for o in layer1 for s in (-1, 1)], count)
    held = distinct(layer0 + [o + s for o in layer0 for s in (-1, 1)], count)
    return layer1, layer0, held


def dot(a, b):
    return jnp.dot(a, b, preferred_element_type=f32)


def pack_kernel(loc, speed, push, kinds, ghosts, lists, counts, inertia, out):
    labels = kinds[...]
    mass = jnp.zeros(labels.shape, f32)
    for s in range(inertia.shape[0]):
        mass = jnp.where(labels == s, inertia[s], mass)
    inv_mass = 1.0 / mass
    atoms, tiles = labels.shape[1], counts.shape[1]
    out[...] = jnp.zeros(out.shape, f32)
    for d in range(3):
        out[d : d + 1, 0:atoms] = (
            loc[d] + time_step * speed[d] + 0.5 * time_step * time_step * push[d] * inv_mass
        )
        out[3 + d : 4 + d, 0:atoms] = speed[d] + 0.5 * time_step * push[d] * inv_mass
    out[6:7, 0:atoms] = labels.astype(f32)
    out[7:8, 0 : ghosts.shape[1]] = ghosts[...].astype(f32)
    out[0:NEI, atoms : atoms + tiles] = lists[0].astype(f32)
    out[NEI : NEI + 1, atoms : atoms + tiles] = counts[...].astype(f32)


def weights_kernel(kind, coef, gain, mix, target, source, wide, columns):
    species = kind.shape[0]
    kinds_f = jnp.transpose(kind[...].astype(f32), (1, 0))
    coef_t = [jnp.transpose(coef[layer], (1, 0)) for layer in range(2)]
    u = []
    for b in range(NB):
        u.append(kinds_f * (coef_t[0][:, b : b + 1] * math.exp(-b * b)))
        columns[b] = jnp.broadcast_to(coef_t[1][:, b : b + 1] * math.exp(-b * b), columns.shape[1:])
    u = jnp.concatenate(u, axis=1)
    high = u.astype(bf16)
    wide[:, 0:TILE] = high
    wide[:, TILE : 2 * TILE] = (u - high.astype(f32)).astype(bf16)
    wide[:, 2 * TILE : 3 * TILE] = high
    gain_t = jnp.transpose(gain[...], (1, 0))
    for layer in range(2):
        columns[NB + layer] = jnp.broadcast_to(gain_t[:, layer : layer + 1], columns.shape[1:])
        wide[:, (3 + 2 * layer) * TILE : (4 + 2 * layer) * TILE] = jnp.transpose(
            mix[layer].astype(f32), (1, 0)
        ).astype(bf16)
    wide[:, 4 * TILE : 5 * TILE] = jnp.concatenate(
        [kinds_f, jnp.zeros((kinds_f.shape[0], TILE - species), f32)], axis=1
    ).astype(bf16)
    both = lax.dot_general(
        source[...], target[...], (((1,), (1,)), ((), ())), preferred_element_type=f32
    )
    high = both.astype(bf16)
    wide[:, 6 * TILE : 7 * TILE] = high
    wide[:, 7 * TILE : 8 * TILE] = (both - high.astype(f32)).astype(bf16)


def lanes_of(parts):
    return jnp.concatenate(parts, axis=1)


def activate(messages, gain):
    messages = messages * UNLIFT
    inverse = lax.rsqrt(jnp.mean(messages * messages, axis=0, keepdims=True) + norm_eps)
    v = messages * inverse * gain
    return (v / (1.0 + jnp.exp(-v))).astype(bf16)


def main_kernel(plan, *refs):
    count, atoms, ghost = plan
    layer1, layer0, held = domain_sets(count)
    tiles = atoms // TILE
    ghost_tiles = ghost // TILE
    ext_tiles = tiles + 2 * ghost_tiles
    n = len(held)
    swaps, levels, taper, inertia = refs[:4]
    refs = refs[4:]
    outside = refs[: n + 2]
    pos_out, vel_out, force_out = refs[n + 2 : n + 5]
    held_data, wide, columns = refs[n + 5 : n + 8]
    arrivals = refs[n + 8]
    data = {o: held_data.at[at] for at, o in enumerate(held)}
    inward = [
        pltpu.make_async_copy(src, dst, arrivals.at[at])
        for at, (src, dst) in enumerate(
            zip(outside, [held_data.at[at] for at in range(n)] + [wide, columns])
        )
    ]
    for c in inward:
        c.start()
    for c in inward[:n]:
        c.wait()
    (
        far_t,
        near_rhs,
        onehot,
        split_pos,
        species_sums,
        ghost_pick,
        hidden1,
        hidden2,
        ext_hidden,
        message_rows,
        envelopes,
        turned,
        asked,
        pulls,
        ints,
        sm,
        sem,
    ) = refs[n + 9 : -2 * BODY]
    basis, squares = refs[-2 * BODY : -BODY], refs[-BODY:]
    u_parts = wide.at[:, 0 : 3 * TILE]
    mix_kind = wide.at[:, 3 * TILE : 4 * TILE + 16]
    mix_second = wide.at[:, 5 * TILE : 6 * TILE]
    both_parts = wide.at[:, 6 * TILE : 8 * TILE]
    kept = basis[0].shape[0]

    for at, o in enumerate(layer0):
        ints[at] = data[o][:, atoms : atoms + TILE].astype(jnp.int32)
    copies = [
        pltpu.make_async_copy(ints.at[at], sm.at[at], sem.at[at]) for at in range(len(layer0))
    ]
    for c in copies:
        c.start()

    row_id = lax.broadcasted_iota(jnp.int32, (8, TILE), 0)
    species_id = lax.broadcasted_iota(jnp.int32, (16, TILE), 0).astype(f32)
    def picked(o, first):
        src = data[o]
        idx = src[7:8, first : first + TILE].astype(jnp.int32)
        idx = jnp.broadcast_to(idx, (8, TILE))
        lane = idx & (TILE - 1)
        block = idx // TILE
        got = jnp.zeros((8, TILE), f32)
        for c in range(tiles):
            here = jnp.take_along_axis(
                src[:, c * TILE : (c + 1) * TILE], lane, axis=1, mode="promise_in_bounds"
            )
            got = jnp.where(block == c, here, got)
        return got

    def thirds(x):
        hi = x.astype(bf16).astype(f32)
        mid = (x - hi).astype(bf16).astype(f32)
        return hi, mid, x - hi - mid

    def rows_of(*rows):
        block = jnp.zeros((8, TILE), f32)
        for r, row in enumerate(rows):
            block = jnp.where(row_id == r, row, block)
        return block

    nowhere = rows_of(1e30, 0.0, 0.0, 1.0, 1.0, 1.0, 1.0)
    blank = jnp.zeros((8, TILE), f32)
    for at in range(len(layer0)):
        far_t[at, ext_tiles] = jnp.transpose(
            jnp.concatenate([blank] * 6 + [nowhere, rows_of(1e30)], axis=0), (1, 0)
        ).astype(bf16)

    for at, o in enumerate(layer0):
        lower, upper = (o - 1) % count, (o + 1) % count
        for e in range(ext_tiles):
            if e < tiles:
                block, shift = data[o][:, e * TILE : (e + 1) * TILE], 0.0
            elif e < tiles + ghost_tiles:
                block, shift = picked(lower, ghost + (e - tiles) * TILE), -slab_width
            else:
                block, shift = picked(upper, (e - tiles - ghost_tiles) * TILE), slab_width
            moved = jnp.where(row_id == 0, block + shift, block) - 0.5 * slab_width
            moved = jnp.where(row_id < 3, moved * SCALE, 0.0)
            onehot[at, e] = jnp.where(species_id == block[6:7, :], 1.0, 0.0).astype(bf16)
            hi, mid, low = thirds(moved)
            size = jnp.sum(moved * moved, axis=0, keepdims=True)
            sizes, steep_sizes = thirds(size), thirds(size * STEEP)
            far_t[at, e] = jnp.transpose(
                jnp.concatenate(
                    [hi, hi, hi, mid, mid, low]
                    + [rows_of(*sizes, 1.0, 1.0, 1.0, 1.0), rows_of(*steep_sizes)],
                    axis=0,
                ),
                (1, 0),
            ).astype(bf16)
            if o == 0:
                split_pos[e] = jnp.concatenate([hi, mid, low, rows_of(1.0)], axis=0).astype(bf16)
            if e < tiles:
                first, second, third = thirds(moved * -2.0)
                power = [-first, -second, -third, -first, -second, -first]
                power += [rows_of(-1.0, -1.0, -1.0, *[-x for x in sizes], TOP), blank]
                first, second, third = thirds(moved * (-2.0 * STEEP))
                steep = [first, second, third, first, second, first]
                steep += [rows_of(0.0, 0.0, 0.0, *steep_sizes), rows_of(1.0, 1.0, 1.0)]
                near_rhs[at, e] = lanes_of(
                    [jnp.concatenate(power, axis=0), jnp.concatenate(steep, axis=0)]
                ).astype(bf16)

    for c in copies:
        c.wait()

    def offsets(at, t):
        far = [
            far_t[at, jnp.where(k < sm[at, NEI, t], sm[at, k, t], ext_tiles)] for k in range(NEI)
        ]
        return dot(jnp.concatenate(far, axis=0), near_rhs[at, t])

    bodies = tiles // BODY
    steps = len(layer0) * bodies

    def basis_step(at, body, u, own):
        t = BODY * body + u
        place = jnp.minimum(at, kept - 1)
        sums = [None] * (NB // 2)
        for half in range(NEI // 2):
            rows = slice(2 * half * TILE, 2 * (half + 1) * TILE)
            lhs = lanes_of([onehot[at, sm[at, 2 * half + k, t]] for k in range(2)])
            power = squares[u][rows, 0:TILE]
            square = jnp.minimum(jnp.maximum(squares[u][rows, TILE : 2 * TILE], 1e-30), FAR)
            slope = square * lax.rsqrt(square)
            ratio = jnp.exp2(slope)
            step = slope + slope
            envelope = None
            for p in range(NB // 2):
                even = jnp.exp2(power)
                odd = even * ratio
                pair = lanes_of([even.astype(bf16), odd.astype(bf16)])
                basis[u][place, body, rows, 2 * p * TILE : 2 * (p + 1) * TILE] = pair
                part = dot(lhs, pair)
                sums[p] = part if half == 0 else sums[p] + part
                if own:
                    part = even * envelope_factor(2 * p) + odd * envelope_factor(2 * p + 1)
                    envelope = part if p == 0 else envelope + part
                if p < NB // 2 - 1:
                    power = power + step
            if own:
                envelopes[t, rows] = envelope
        sums = [x[:, k * TILE : (k + 1) * TILE] for x in sums for k in range(2)]
        sums = jnp.concatenate(sums, axis=0)
        high = sums.astype(bf16)
        low = (sums - high.astype(f32)).astype(bf16)
        species_sums[at, t] = jnp.concatenate([high, high, low], axis=0)

    def envelope_factor(b):
        return taper[b] * (math.exp(-b * b) * UNLIFT / (math.sqrt(TILE * NEI * TILE) * SCALE))

    def first_layer(at):
        messages = dot(u_parts[...], lanes_of([species_sums[at, t] for t in range(tiles)]))
        activations = [
            activate(messages[:, t * TILE : (t + 1) * TILE], columns[NB]) for t in range(tiles)
        ]
        kinds = lanes_of([onehot[at, t] for t in range(tiles)])
        hidden = dot(mix_kind[...], jnp.concatenate([lanes_of(activations), kinds], axis=0))
        for t in range(tiles):
            hidden1[at, t] = hidden[:, t * TILE : (t + 1) * TILE].astype(bf16)

    squares[0][...] = offsets(0, 0)

    def body_step(own, m, _):
        at, body = m // bodies, m % bodies
        after = jnp.minimum(m + 1, steps - 1)
        for u in range(BODY):
            if u == BODY - 1:
                upcoming = offsets(after // bodies, BODY * (after % bodies))
            else:
                upcoming = offsets(at, BODY * body + u + 1)
            basis_step(at, body, u, own)
            squares[(u + 1) % BODY][...] = upcoming
        return 0

    for c in inward[n:]:
        c.wait()
    lax.fori_loop(0, bodies, functools.partial(body_step, True), 0)
    lax.fori_loop(bodies, steps, functools.partial(body_step, False), 0)

    for at, o in enumerate(layer0):
        chosen = data[o][7:8, 0 : 2 * ghost]

        def pick_step(c, _):
            first = pl.multiple_of(c * TILE, TILE)
            rows = lax.broadcasted_iota(jnp.int32, (TILE, 2 * ghost), 0) + first
            ghost_pick[at, pl.ds(first, TILE), :] = jnp.where(
                rows.astype(f32) == chosen, 1.0, 0.0
            ).astype(bf16)
            return 0

        lax.fori_loop(0, tiles, pick_step, 0)

    for at in range(len(layer0)):
        first_layer(at)

    def extend(target, source_hidden, sets, o):
        for side, other in ((0, (o - 1) % count), (1, (o + 1) % count)):
            at = sets.index(other)
            rows = lanes_of([source_hidden[at, t] for t in range(tiles)])
            first = ghost if side == 0 else 0
            got = dot(
                rows, ghost_pick[layer0.index(other), :, first : first + ghost]
            ).astype(bf16)
            for g in range(ghost_tiles):
                target[tiles + side * ghost_tiles + g] = got[:, g * TILE : (g + 1) * TILE]

    def second_step(keep, t):
        at = layer0.index(layer1[keep])
        lhs = lanes_of([ext_hidden[keep, sm[at, k, t]] for k in range(NEI)])
        sums = dot(lhs, basis[t % BODY][keep, t // BODY])
        messages = None
        for b in range(NB):
            part = sums[:, b * TILE : (b + 1) * TILE] * columns[b]
            messages = part if messages is None else messages + part
        message_rows[keep, t] = messages

    def finish_second(keep, activations):
        at = layer0.index(layer1[keep])
        added = dot(mix_second[...], lanes_of(activations))
        for t in range(tiles):
            block = hidden1[at, t].astype(f32) + added[:, t * TILE : (t + 1) * TILE]
            hidden2[keep, t] = block.astype(bf16)

    def turn(block):
        return jnp.transpose(block.astype(f32), (1, 0)).astype(bf16)

    def import_final():
        extend(last, hidden2, layer1, 0)
        for e in range(tiles, ext_tiles):
            turned[e] = turn(last[e])

    last = ext_hidden.at[len(layer1)]
    order = list(range(1, len(layer1))) + [0]
    for keep in order:
        o = layer1[keep]
        for t in range(tiles):
            ext_hidden[keep, t] = hidden1[layer0.index(o), t]
        extend(ext_hidden.at[keep], hidden1, layer0, o)
    pending = []
    for keep in order:
        activations = []
        for t in range(tiles):
            second_step(keep, t)
            if t:
                activations.append(activate(message_rows[keep, t - 1], columns[NB + 1]))
            if pending and t % 2:
                pending.pop(0)()
        activations.append(activate(message_rows[keep, tiles - 1], columns[NB + 1]))
        for job in pending:
            job()
        pending = [functools.partial(finish_second, keep, activations)]
        if keep and keep == order[-2]:
            pending.append(import_final)
    for job in pending:
        job()
    if len(order) == 1:
        import_final()
    own_hidden = [hidden2[0, t] for t in range(tiles)]
    for t in range(tiles):
        turned[t] = turn(own_hidden[t])
    own_hidden = lanes_of(own_hidden)
    wanted = dot(both_parts[...], jnp.concatenate([own_hidden, own_hidden], axis=0)).astype(bf16)
    for t in range(tiles):
        asked[t] = wanted[:, t * TILE : (t + 1) * TILE]

    for t in range(tiles):
        lhs = jnp.concatenate([turned[sm[0, k, t]] for k in range(NEI)], axis=0)
        weight = (dot(lhs, asked[t]) * envelopes[t]).astype(bf16)
        places = lanes_of([split_pos[sm[0, k, t]] for k in range(NEI)])
        got = dot(places, weight)
        pulls[t] = jnp.concatenate([got[0:8] + got[8:16] + got[16:24], got[24:32]], axis=0)

    me = lax.axis_index("rep")
    quotient = jnp.sqrt(
        jnp.full((1, TILE), levels[me], f32) / jnp.full((1, TILE), levels[swaps[me]], f32)
    )
    own = data[0]
    labels = own[6:7, 0:atoms]
    mass = jnp.zeros(labels.shape, f32)
    for s in range(inertia.shape[0]):
        mass = jnp.where(labels == s, inertia[s], mass)
    inv_mass = 1.0 / mass
    for t in range(tiles):
        lanes = slice(t * TILE, (t + 1) * TILE)
        got = pulls[t]
        force = got[0:8] - (own[:, lanes] - 0.5 * slab_width) * SCALE * got[8:9]
        velocity = own[3:6, lanes] + 0.5 * time_step * force[0:3] * inv_mass[:, lanes]
        velocity = velocity * quotient
        for d in range(3):
            pos_out[d, :, lanes] = own[d : d + 1, lanes]
            force_out[d, :, lanes] = force[d : d + 1]
            vel_out[d, :, lanes] = velocity[d : d + 1]


def local(
    count,
    replicas,
    particle_locations,
    particle_speeds,
    current_pushes,
    particle_kinds,
    halo_particle_labels,
    adjacent_block_labels,
    adjacent_place_totals,
    kind_vectors,
    kind_inertia,
    stepwise_distance_coefficients,
    signal_scaling_factors,
    feature_blend_coefficients,
    target_projection_array,
    source_projection_array,
    push_distance_taper,
    thermal_levels,
    granted_swaps,
):
    atoms = particle_locations.shape[2]
    ghost = halo_particle_labels.shape[1] // 2
    channels = kind_vectors.shape[1]
    tiles = atoms // TILE
    ext_tiles = tiles + 2 * (ghost // TILE)
    layer1, layer0, held = domain_sets(count)
    vmem = pl.BlockSpec(memory_space=pltpu.VMEM)
    smem = pl.BlockSpec(memory_space=pltpu.SMEM)
    shape = jax.ShapeDtypeStruct

    packed = pl.pallas_call(
        pack_kernel,
        out_shape=shape((8, atoms + TILE), f32),
        in_specs=[vmem] * 7 + [smem],
        out_specs=vmem,
    )(
        jnp.transpose(particle_locations, (1, 0, 2)),
        jnp.transpose(particle_speeds, (1, 0, 2)),
        jnp.transpose(current_pushes, (1, 0, 2)),
        particle_kinds,
        halo_particle_labels,
        jnp.transpose(adjacent_block_labels, (0, 2, 1)),
        adjacent_place_totals,
        kind_inertia,
    )

    even = [(i, i ^ 1) for i in range(replicas)]
    odd = [(i, ((i + 1) ^ 1) - 1) for i in range(1, replicas - 1)]
    odd_all = [(a * count + d, b * count + d) for a, b in odd for d in range(count)] + [
        (r * count + d, r * count + (d + 1) % count) for r in (0, replicas - 1) for d in range(count)
    ]
    from_even = lax.ppermute(packed, "rep", even)
    from_odd = lax.ppermute(packed, ("rep", "dom"), odd_all)
    me = lax.axis_index("rep")
    partner = granted_swaps[me]
    low = jnp.minimum(me, partner)
    chosen = jnp.where(partner == me, packed, jnp.where(low % 2 == 0, from_even, from_odd))
    data = [
        chosen
        if o == 0
        else lax.ppermute(chosen, "dom", [((d + o) % count, d) for d in range(count)])
        for o in held
    ]

    weights = pl.pallas_call(
        weights_kernel,
        out_shape=[shape((channels, 8 * TILE), bf16), shape((NB + 2, channels, TILE), f32)],
        in_specs=[vmem] * 6,
        out_specs=[vmem] * 2,
        cost_estimate=pl.CostEstimate(flops=10**6, bytes_accessed=10**6, transcendentals=0),
    )(
        kind_vectors,
        stepwise_distance_coefficients,
        signal_scaling_factors,
        feature_blend_coefficients,
        target_projection_array,
        source_projection_array,
    )

    n0, n1 = len(layer0), len(layer1)
    kept = (n1 + (n0 > n1), tiles // BODY, NEI * TILE, NB * TILE)
    buffers = [
        ((n0, ext_tiles + 1, TILE, 64), bf16),
        ((n0, tiles, 64, 2 * TILE), bf16),
        ((n0, ext_tiles, 16, TILE), bf16),
        ((ext_tiles, 32, TILE), bf16),
        ((n0, tiles, 3 * NB * 16, TILE), bf16),
        ((n0, atoms, 2 * ghost), bf16),
        ((n0, tiles, TILE, TILE), bf16),
        ((n1, tiles, TILE, TILE), bf16),
        ((n1 + 1, ext_tiles, TILE, TILE), bf16),
        ((n1, tiles, TILE, TILE), f32),
        ((tiles, NEI * TILE, TILE), f32),
        ((ext_tiles, TILE, TILE), bf16),
        ((tiles, TILE, TILE), bf16),
        ((tiles, 16, TILE), f32),
        ((n0, 8, TILE), jnp.int32),
    ]
    scratch = [
        pltpu.VMEM((len(held), 8, atoms + TILE), f32),
        pltpu.VMEM((channels, 8 * TILE), bf16),
        pltpu.VMEM((NB + 2, channels, TILE), f32),
        pltpu.SemaphoreType.DMA((len(held) + 2,)),
    ]
    scratch += [pltpu.VMEM(*buffer) for buffer in buffers] + [
        pltpu.SMEM((n0, 8, TILE), jnp.int32),
        pltpu.SemaphoreType.DMA((n0,)),
    ]
    scratch += [pltpu.VMEM(kept, bf16)] * BODY
    scratch += [pltpu.VMEM((NEI * TILE, 2 * TILE), f32)] * BODY

    outs = pl.pallas_call(
        functools.partial(main_kernel, (count, atoms, ghost)),
        out_shape=[shape((3, 1, atoms), f32)] * 3,
        in_specs=[smem] * 4 + [pl.BlockSpec(memory_space=pl.ANY)] * (len(held) + 2),
        out_specs=[vmem] * 3,
        scratch_shapes=scratch,
        compiler_params=pltpu.CompilerParams(vmem_limit_bytes=58 * 2**20),
    )(
        granted_swaps,
        thermal_levels,
        push_distance_taper,
        kind_inertia,
        *data,
        *weights,
    )
    return tuple(jnp.transpose(x, (1, 0, 2)) for x in outs)


def solution(mesh):
    in_specs = (
        P("rep", None, "dom"),
        P("rep", None, "dom"),
        P("rep", None, "dom"),
        P("rep", "dom"),
        P("rep", "dom"),
        P("rep", "dom", None),
        P("rep", "dom"),
    ) + (P(),) * 10
    out_specs = (P("rep", None, "dom"), P("rep", None, "dom"), P("rep", None, "dom"))
    step = functools.partial(local, mesh.shape["dom"], mesh.shape["rep"])
    return jax.shard_map(step, mesh=mesh, in_specs=in_specs, out_specs=out_specs, check_vma=False)
```

```python
import functools
import math

import jax
import jax.numpy as jnp
from jax import lax
from jax.experimental import pallas as pl
from jax.experimental.pallas import tpu as pltpu
from jax.sharding import PartitionSpec as P

NB = 8
TILE = 128
NEI = 4

slab_width = 1.5
time_step = 0.5
basis_width = 0.3
norm_eps = 1e-06

f32 = jnp.float32
bf16 = jnp.bfloat16

LOG2E = math.log2(math.e)
SCALE = math.sqrt(LOG2E) / basis_width
TOP = 34.0
UNLIFT = 2.0**-TOP
STEEP = 4.0 * LOG2E
FAR = (40.0 * LOG2E) ** 2
BODY = 4


def distinct(offsets, count):
    return list(dict.fromkeys(o % count for o in offsets))


def domain_sets(count):
    layer1 = distinct([0, -1, 1], count)
    layer0 = distinct(layer1 + [o + s for o in layer1 for s in (-1, 1)], count)
    held = distinct(layer0 + [o + s for o in layer0 for s in (-1, 1)], count)
    return layer1, layer0, held


def dot(a, b):
    return jnp.dot(a, b, preferred_element_type=f32)


def pack_kernel(loc, speed, push, kinds, ghosts, lists, counts, inertia, out):
    labels = kinds[...]
    mass = jnp.zeros(labels.shape, f32)
    for s in range(inertia.shape[0]):
        mass = jnp.where(labels == s, inertia[s], mass)
    inv_mass = 1.0 / mass
    atoms, tiles = labels.shape[1], counts.shape[1]
    out[...] = jnp.zeros(out.shape, f32)
    for d in range(3):
        out[d : d + 1, 0:atoms] = (
            loc[d] + time_step * speed[d] + 0.5 * time_step * time_step * push[d] * inv_mass
        )
        out[3 + d : 4 + d, 0:atoms] = speed[d] + 0.5 * time_step * push[d] * inv_mass
    out[6:7, 0:atoms] = labels.astype(f32)
    out[7:8, 0 : ghosts.shape[1]] = ghosts[...].astype(f32)
    out[0:NEI, atoms : atoms + tiles] = lists[0].astype(f32)
    out[NEI : NEI + 1, atoms : atoms + tiles] = counts[...].astype(f32)


def weights_kernel(
    kind, coef, gain, mix, target, source, swaps, levels, taper, inertia, wide, columns, small
):
    me = lax.axis_index("rep")
    lane = lax.broadcasted_iota(jnp.int32, (1, TILE), 1)
    factors, masses = jnp.zeros((1, TILE), f32), jnp.zeros((1, TILE), f32)
    for b in range(NB):
        scale = math.exp(-b * b) * UNLIFT / (math.sqrt(TILE * NEI * TILE) * SCALE)
        factors = jnp.where(lane == b, taper[b] * scale, factors)
    for s in range(inertia.shape[0]):
        masses = jnp.where(lane == s, inertia[s], masses)
    quotient = jnp.full((1, TILE), levels[me], f32) / jnp.full((1, TILE), levels[swaps[me]], f32)
    small[0:1] = factors
    small[1:2] = masses
    small[2:3] = jnp.sqrt(quotient)
    small[3:8] = jnp.zeros((5, TILE), f32)
    species = kind.shape[0]
    kinds_f = jnp.transpose(kind[...].astype(f32), (1, 0))
    coef_t = [jnp.transpose(coef[layer], (1, 0)) for layer in range(2)]
    u = []
    for b in range(NB):
        u.append(kinds_f * (coef_t[0][:, b : b + 1] * math.exp(-b * b)))
        columns[b] = jnp.broadcast_to(coef_t[1][:, b : b + 1] * math.exp(-b * b), columns.shape[1:])
    u = jnp.concatenate(u, axis=1)
    high = u.astype(bf16)
    wide[:, 0:TILE] = high
    wide[:, TILE : 2 * TILE] = (u - high.astype(f32)).astype(bf16)
    wide[:, 2 * TILE : 3 * TILE] = high
    gain_t = jnp.transpose(gain[...], (1, 0))
    for layer in range(2):
        columns[NB + layer] = jnp.broadcast_to(gain_t[:, layer : layer + 1], columns.shape[1:])
        wide[:, (3 + 2 * layer) * TILE : (4 + 2 * layer) * TILE] = jnp.transpose(
            mix[layer].astype(f32), (1, 0)
        ).astype(bf16)
    wide[:, 4 * TILE : 5 * TILE] = jnp.concatenate(
        [kinds_f, jnp.zeros((kinds_f.shape[0], TILE - species), f32)], axis=1
    ).astype(bf16)
    both = lax.dot_general(
        source[...], target[...], (((1,), (1,)), ((), ())), preferred_element_type=f32
    )
    high = both.astype(bf16)
    wide[:, 6 * TILE : 7 * TILE] = high
    wide[:, 7 * TILE : 8 * TILE] = (both - high.astype(f32)).astype(bf16)


def lanes_of(parts):
    return jnp.concatenate(parts, axis=1)


def activate(messages, gain):
    messages = messages * UNLIFT
    inverse = lax.rsqrt(jnp.mean(messages * messages, axis=0, keepdims=True) + norm_eps)
    v = messages * inverse * gain
    return (v / (1.0 + jnp.exp(-v))).astype(bf16)


def main_kernel(plan, *refs):
    count, atoms, ghost, species = plan
    layer1, layer0, held = domain_sets(count)
    tiles = atoms // TILE
    ghost_tiles = ghost // TILE
    ext_tiles = tiles + 2 * ghost_tiles
    n = len(held)
    outside = refs[: n + 3]
    outputs = refs[n + 3 : n + 6]
    held_data, wide, columns, small = refs[n + 6 : n + 10]
    pos_out, vel_out, force_out, arrivals, departures = refs[n + 10 : n + 15]
    data = {o: held_data.at[at] for at, o in enumerate(held)}
    inward = [
        pltpu.make_async_copy(src, dst, arrivals.at[at])
        for at, (src, dst) in enumerate(
            zip(outside, [held_data.at[at] for at in range(n)] + [wide, columns, small])
        )
    ]
    for c in inward:
        c.start()
    for c in inward[:n]:
        c.wait()
    (
        far_t,
        near_rhs,
        onehot,
        split_pos,
        species_sums,
        ghost_pick,
        hidden1,
        hidden2,
        ext_hidden,
        message_rows,
        envelopes,
        turned,
        asked,
        pulls,
        ints,
        sm,
        sem,
    ) = refs[n + 15 : -2 * BODY]
    basis, squares = refs[-2 * BODY : -BODY], refs[-BODY:]
    u_parts = wide.at[:, 0 : 3 * TILE]
    mix_kind = wide.at[:, 3 * TILE : 4 * TILE + 16]
    mix_second = wide.at[:, 5 * TILE : 6 * TILE]
    both_parts = wide.at[:, 6 * TILE : 8 * TILE]
    kept = basis[0].shape[0]

    for at, o in enumerate(layer0):
        ints[at] = data[o][:, atoms : atoms + TILE].astype(jnp.int32)
    copies = [
        pltpu.make_async_copy(ints.at[at], sm.at[at], sem.at[at]) for at in range(len(layer0))
    ]
    for c in copies:
        c.start()

    outward = [
        pltpu.make_async_copy(src, dst, departures.at[at])
        for at, (src, dst) in enumerate(zip((pos_out, vel_out, force_out), outputs))
    ]
    for d in range(3):
        pos_out[d] = data[0][d : d + 1, 0:atoms]
    outward[0].start()

    row_id = lax.broadcasted_iota(jnp.int32, (8, TILE), 0)
    species_id = lax.broadcasted_iota(jnp.int32, (16, TILE), 0).astype(f32)
    def picked(o, first):
        src = data[o]
        idx = src[7:8, first : first + TILE].astype(jnp.int32)
        idx = jnp.broadcast_to(idx, (8, TILE))
        lane = idx & (TILE - 1)
        block = idx // TILE
        got = jnp.zeros((8, TILE), f32)
        for c in range(tiles):
            here = jnp.take_along_axis(
                src[:, c * TILE : (c + 1) * TILE], lane, axis=1, mode="promise_in_bounds"
            )
            got = jnp.where(block == c, here, got)
        return got

    def thirds(x):
        hi = x.astype(bf16).astype(f32)
        mid = (x - hi).astype(bf16).astype(f32)
        return hi, mid, x - hi - mid

    def rows_of(*rows):
        block = jnp.zeros((8, TILE), f32)
        for r, row in enumerate(rows):
            block = jnp.where(row_id == r, row, block)
        return block

    nowhere = rows_of(1e30, 0.0, 0.0, 1.0, 1.0, 1.0, 1.0)
    blank = jnp.zeros((8, TILE), f32)
    for at in range(len(layer0)):
        far_t[at, ext_tiles] = jnp.transpose(
            jnp.concatenate([blank] * 6 + [nowhere, rows_of(1e30)], axis=0), (1, 0)
        ).astype(bf16)

    for at, o in enumerate(layer0):
        lower, upper = (o - 1) % count, (o + 1) % count
        for e in range(ext_tiles):
            if e < tiles:
                block, shift = data[o][:, e * TILE : (e + 1) * TILE], 0.0
            elif e < tiles + ghost_tiles:
                block, shift = picked(lower, ghost + (e - tiles) * TILE), -slab_width
            else:
                block, shift = picked(upper, (e - tiles - ghost_tiles) * TILE), slab_width
            moved = jnp.where(row_id == 0, block + shift, block) - 0.5 * slab_width
            moved = jnp.where(row_id < 3, moved * SCALE, 0.0)
            onehot[at, e] = jnp.where(species_id == block[6:7, :], 1.0, 0.0).astype(bf16)
            hi, mid, low = thirds(moved)
            size = jnp.sum(moved * moved, axis=0, keepdims=True)
            sizes, steep_sizes = thirds(size), thirds(size * STEEP)
            far_t[at, e] = jnp.transpose(
                jnp.concatenate(
                    [hi, hi, hi, mid, mid, low]
                    + [rows_of(*sizes, 1.0, 1.0, 1.0, 1.0), rows_of(*steep_sizes)],
                    axis=0,
                ),
                (1, 0),
            ).astype(bf16)
            if o == 0:
                split_pos[e] = jnp.concatenate([hi, mid, low, rows_of(1.0)], axis=0).astype(bf16)
            if e < tiles:
                first, second, third = thirds(moved * -2.0)
                power = [-first, -second, -third, -first, -second, -first]
                power += [rows_of(-1.0, -1.0, -1.0, *[-x for x in sizes], TOP), blank]
                first, second, third = thirds(moved * (-2.0 * STEEP))
                steep = [first, second, third, first, second, first]
                steep += [rows_of(0.0, 0.0, 0.0, *steep_sizes), rows_of(1.0, 1.0, 1.0)]
                near_rhs[at, e] = lanes_of(
                    [jnp.concatenate(power, axis=0), jnp.concatenate(steep, axis=0)]
                ).astype(bf16)

    for c in copies:
        c.wait()

    def offsets(at, t):
        far = [
            far_t[at, jnp.where(k < sm[at, NEI, t], sm[at, k, t], ext_tiles)] for k in range(NEI)
        ]
        return dot(jnp.concatenate(far, axis=0), near_rhs[at, t])

    bodies = tiles // BODY
    steps = len(layer0) * bodies

    def basis_step(at, body, u, own):
        t = BODY * body + u
        place = jnp.minimum(at, kept - 1)
        sums = [None] * (NB // 2)
        for half in range(NEI // 2):
            rows = slice(2 * half * TILE, 2 * (half + 1) * TILE)
            lhs = lanes_of([onehot[at, sm[at, 2 * half + k, t]] for k in range(2)])
            power = squares[u][rows, 0:TILE]
            square = jnp.minimum(jnp.maximum(squares[u][rows, TILE : 2 * TILE], 1e-30), FAR)
            slope = square * lax.rsqrt(square)
            ratio = jnp.exp2(slope)
            step = slope + slope
            envelope = None
            for p in range(NB // 2):
                even = jnp.exp2(power)
                odd = even * ratio
                pair = lanes_of([even.astype(bf16), odd.astype(bf16)])
                basis[u][place, body, rows, 2 * p * TILE : 2 * (p + 1) * TILE] = pair
                part = dot(lhs, pair)
                sums[p] = part if half == 0 else sums[p] + part
                if own:
                    part = even * small[0, 2 * p] + odd * small[0, 2 * p + 1]
                    envelope = part if p == 0 else envelope + part
                if p < NB // 2 - 1:
                    power = power + step
            if own:
                envelopes[t, rows] = envelope
        sums = [x[:, k * TILE : (k + 1) * TILE] for x in sums for k in range(2)]
        sums = jnp.concatenate(sums, axis=0)
        high = sums.astype(bf16)
        low = (sums - high.astype(f32)).astype(bf16)
        species_sums[at, t] = jnp.concatenate([high, high, low], axis=0)

    def first_layer(at):
        messages = dot(u_parts[...], lanes_of([species_sums[at, t] for t in range(tiles)]))
        activations = [
            activate(messages[:, t * TILE : (t + 1) * TILE], columns[NB]) for t in range(tiles)
        ]
        kinds = lanes_of([onehot[at, t] for t in range(tiles)])
        hidden = dot(mix_kind[...], jnp.concatenate([lanes_of(activations), kinds], axis=0))
        for t in range(tiles):
            hidden1[at, t] = hidden[:, t * TILE : (t + 1) * TILE].astype(bf16)

    squares[0][...] = offsets(0, 0)

    def body_step(own, m, _):
        at, body = m // bodies, m % bodies
        after = jnp.minimum(m + 1, steps - 1)
        for u in range(BODY):
            if u == BODY - 1:
                upcoming = offsets(after // bodies, BODY * (after % bodies))
            else:
                upcoming = offsets(at, BODY * body + u + 1)
            basis_step(at, body, u, own)
            squares[(u + 1) % BODY][...] = upcoming
        return 0

    for c in inward[n:]:
        c.wait()
    lax.fori_loop(0, bodies, functools.partial(body_step, True), 0)
    lax.fori_loop(bodies, steps, functools.partial(body_step, False), 0)

    for at, o in enumerate(layer0):
        chosen = data[o][7:8, 0 : 2 * ghost]

        def pick_step(c, _):
            first = pl.multiple_of(c * TILE, TILE)
            rows = lax.broadcasted_iota(jnp.int32, (TILE, 2 * ghost), 0) + first
            ghost_pick[at, pl.ds(first, TILE), :] = jnp.where(
                rows.astype(f32) == chosen, 1.0, 0.0
            ).astype(bf16)
            return 0

        lax.fori_loop(0, tiles, pick_step, 0)

    for at in range(len(layer0)):
        first_layer(at)

    def extend(target, source_hidden, sets, o):
        for side, other in ((0, (o - 1) % count), (1, (o + 1) % count)):
            at = sets.index(other)
            rows = lanes_of([source_hidden[at, t] for t in range(tiles)])
            first = ghost if side == 0 else 0
            got = dot(
                rows, ghost_pick[layer0.index(other), :, first : first + ghost]
            ).astype(bf16)
            for g in range(ghost_tiles):
                target[tiles + side * ghost_tiles + g] = got[:, g * TILE : (g + 1) * TILE]

    def second_step(keep, t):
        at = layer0.index(layer1[keep])
        lhs = lanes_of([ext_hidden[keep, sm[at, k, t]] for k in range(NEI)])
        sums = dot(lhs, basis[t % BODY][keep, t // BODY])
        messages = None
        for b in range(NB):
            part = sums[:, b * TILE : (b + 1) * TILE] * columns[b]
            messages = part if messages is None else messages + part
        message_rows[keep, t] = messages

    def finish_second(keep, activations):
        at = layer0.index(layer1[keep])
        added = dot(mix_second[...], lanes_of(activations))
        for t in range(tiles):
            block = hidden1[at, t].astype(f32) + added[:, t * TILE : (t + 1) * TILE]
            hidden2[keep, t] = block.astype(bf16)

    def turn(block):
        return jnp.transpose(block.astype(f32), (1, 0)).astype(bf16)

    def import_final():
        extend(last, hidden2, layer1, 0)
        for e in range(tiles, ext_tiles):
            turned[e] = turn(last[e])

    last = ext_hidden.at[len(layer1)]
    order = list(range(1, len(layer1))) + [0]
    for keep in order:
        o = layer1[keep]
        for t in range(tiles):
            ext_hidden[keep, t] = hidden1[layer0.index(o), t]
        extend(ext_hidden.at[keep], hidden1, layer0, o)
    pending = []
    for keep in order:
        activations = []
        for t in range(tiles):
            second_step(keep, t)
            if t:
                activations.append(activate(message_rows[keep, t - 1], columns[NB + 1]))
            if pending and t % 2:
                pending.pop(0)()
        activations.append(activate(message_rows[keep, tiles - 1], columns[NB + 1]))
        for job in pending:
            job()
        pending = [functools.partial(finish_second, keep, activations)]
        if keep and keep == order[-2]:
            pending.append(import_final)
    for job in pending:
        job()
    if len(order) == 1:
        import_final()
    own_hidden = [hidden2[0, t] for t in range(tiles)]
    for t in range(tiles):
        turned[t] = turn(own_hidden[t])
    own_hidden = lanes_of(own_hidden)
    wanted = dot(both_parts[...], jnp.concatenate([own_hidden, own_hidden], axis=0)).astype(bf16)
    empty = jnp.zeros((TILE, TILE), bf16)
    duos = range(tiles // 2)
    for q in duos:
        first, second = (wanted[:, t * TILE : (t + 1) * TILE] for t in (2 * q, 2 * q + 1))
        asked[q] = jnp.concatenate([lanes_of([first, empty]), lanes_of([empty, second])], axis=0)

    def weigh(q):
        lhs = [lanes_of([turned[sm[0, k, t]] for t in (2 * q, 2 * q + 1)]) for k in range(NEI)]
        scores = dot(jnp.concatenate(lhs, axis=0), asked[q])
        return (scores * lanes_of([envelopes[t] for t in (2 * q, 2 * q + 1)])).astype(bf16)

    def pull(q, weight):
        places = [
            lanes_of([split_pos[sm[0, k, t]] for k in range(NEI)]) for t in (2 * q, 2 * q + 1)
        ]
        got = dot(jnp.concatenate(places, axis=0), weight)
        for side in range(2):
            part = got[32 * side : 32 * (side + 1), side * TILE : (side + 1) * TILE]
            pulls[2 * q + side] = jnp.concatenate(
                [part[0:8] + part[8:16] + part[16:24], part[24:32]], axis=0
            )

    weights = {0: weigh(0)}
    for q in duos:
        if q + 1 in duos:
            weights[q + 1] = weigh(q + 1)
        pull(q, weights.pop(q))

    own = data[0]
    labels = own[6:7, 0:atoms]
    mass = jnp.zeros(labels.shape, f32)
    for s in range(species):
        mass = jnp.where(labels == s, small[1, s], mass)
    inv_mass = 1.0 / mass
    for t in range(tiles):
        lanes = slice(t * TILE, (t + 1) * TILE)
        got = pulls[t]
        force = got[0:8] - (own[:, lanes] - 0.5 * slab_width) * SCALE * got[8:9]
        velocity = own[3:6, lanes] + 0.5 * time_step * force[0:3] * inv_mass[:, lanes]
        velocity = velocity * small[2, 0]
        for d in range(3):
            force_out[d, :, lanes] = force[d : d + 1]
            vel_out[d, :, lanes] = velocity[d : d + 1]
    for c in outward[1:]:
        c.start()
    for c in outward:
        c.wait()


def local(
    count,
    replicas,
    particle_locations,
    particle_speeds,
    current_pushes,
    particle_kinds,
    halo_particle_labels,
    adjacent_block_labels,
    adjacent_place_totals,
    kind_vectors,
    kind_inertia,
    stepwise_distance_coefficients,
    signal_scaling_factors,
    feature_blend_coefficients,
    target_projection_array,
    source_projection_array,
    push_distance_taper,
    thermal_levels,
    granted_swaps,
):
    atoms = particle_locations.shape[2]
    ghost = halo_particle_labels.shape[1] // 2
    channels = kind_vectors.shape[1]
    tiles = atoms // TILE
    ext_tiles = tiles + 2 * (ghost // TILE)
    layer1, layer0, held = domain_sets(count)
    vmem = pl.BlockSpec(memory_space=pltpu.VMEM)
    smem = pl.BlockSpec(memory_space=pltpu.SMEM)
    shape = jax.ShapeDtypeStruct

    packed = pl.pallas_call(
        pack_kernel,
        out_shape=shape((8, atoms + TILE), f32),
        in_specs=[vmem] * 7 + [smem],
        out_specs=vmem,
    )(
        jnp.transpose(particle_locations, (1, 0, 2)),
        jnp.transpose(particle_speeds, (1, 0, 2)),
        jnp.transpose(current_pushes, (1, 0, 2)),
        particle_kinds,
        halo_particle_labels,
        jnp.transpose(adjacent_block_labels, (0, 2, 1)),
        adjacent_place_totals,
        kind_inertia,
    )

    even = [(i, i ^ 1) for i in range(replicas)]
    odd = [(i, ((i + 1) ^ 1) - 1) for i in range(1, replicas - 1)]
    odd_all = [(a * count + d, b * count + d) for a, b in odd for d in range(count)] + [
        (r * count + d, r * count + (d + 1) % count) for r in (0, replicas - 1) for d in range(count)
    ]
    from_even = lax.ppermute(packed, "rep", even)
    from_odd = lax.ppermute(packed, ("rep", "dom"), odd_all)
    me = lax.axis_index("rep")
    partner = granted_swaps[me]
    low = jnp.minimum(me, partner)
    chosen = jnp.where(partner == me, packed, jnp.where(low % 2 == 0, from_even, from_odd))
    data = [
        chosen
        if o == 0
        else lax.ppermute(chosen, "dom", [((d + o) % count, d) for d in range(count)])
        for o in held
    ]

    weights = pl.pallas_call(
        weights_kernel,
        out_shape=[
            shape((channels, 8 * TILE), bf16),
            shape((NB + 2, channels, TILE), f32),
            shape((8, TILE), f32),
        ],
        in_specs=[vmem] * 6 + [smem] * 4,
        out_specs=[vmem] * 3,
        compiler_params=pltpu.CompilerParams(vmem_limit_bytes=8 * 2**20),
        cost_estimate=pl.CostEstimate(flops=10**6, bytes_accessed=10**6, transcendentals=0),
    )(
        kind_vectors,
        stepwise_distance_coefficients,
        signal_scaling_factors,
        feature_blend_coefficients,
        target_projection_array,
        source_projection_array,
        granted_swaps,
        thermal_levels,
        push_distance_taper,
        kind_inertia,
    )

    n0, n1 = len(layer0), len(layer1)
    kept = (n1 + (n0 > n1), tiles // BODY, NEI * TILE, NB * TILE)
    buffers = [
        ((n0, ext_tiles + 1, TILE, 64), bf16),
        ((n0, tiles, 64, 2 * TILE), bf16),
        ((n0, ext_tiles, 16, TILE), bf16),
        ((ext_tiles, 32, TILE), bf16),
        ((n0, tiles, 3 * NB * 16, TILE), bf16),
        ((n0, atoms, 2 * ghost), bf16),
        ((n0, tiles, TILE, TILE), bf16),
        ((n1, tiles, TILE, TILE), bf16),
        ((n1 + 1, ext_tiles, TILE, TILE), bf16),
        ((n1, tiles, TILE, TILE), f32),
        ((tiles, NEI * TILE, TILE), f32),
        ((ext_tiles, TILE, TILE), bf16),
        ((tiles // 2, 2 * TILE, 2 * TILE), bf16),
        ((tiles, 16, TILE), f32),
        ((n0, 8, TILE), jnp.int32),
    ]
    inner = [
        ((len(held), 8, atoms + TILE), f32),
        ((channels, 8 * TILE), bf16),
        ((NB + 2, channels, TILE), f32),
    ]
    outgoing = [((3, 1, atoms), f32)] * 3
    outer = [(kept, bf16)] * BODY + [((NEI * TILE, 2 * TILE), f32)] * BODY
    scratch = [pltpu.VMEM(*buffer) for buffer in inner] + [pltpu.SMEM((8, TILE), f32)]
    scratch += [pltpu.VMEM(*buffer) for buffer in outgoing]
    scratch += [pltpu.SemaphoreType.DMA((len(held) + 3,)), pltpu.SemaphoreType.DMA((3,))]
    scratch += [pltpu.VMEM(*buffer) for buffer in buffers] + [
        pltpu.SMEM((n0, 8, TILE), jnp.int32),
        pltpu.SemaphoreType.DMA((n0,)),
    ]
    scratch += [pltpu.VMEM(*buffer) for buffer in outer]
    limit = 6 * 2**20 + sum(
        math.prod(dims[:-1]) * max(dims[-1], TILE) * jnp.dtype(kind).itemsize
        for dims, kind in inner + outgoing + buffers + outer
    )

    outs = pl.pallas_call(
        functools.partial(main_kernel, (count, atoms, ghost, kind_vectors.shape[0])),
        out_shape=[shape((3, 1, atoms), f32)] * 3,
        in_specs=[pl.BlockSpec(memory_space=pl.ANY)] * (len(held) + 3),
        out_specs=[pl.BlockSpec(memory_space=pl.ANY)] * 3,
        scratch_shapes=scratch,
        compiler_params=pltpu.CompilerParams(vmem_limit_bytes=limit),
    )(
        *data,
        *weights,
    )
    return tuple(jnp.transpose(x, (1, 0, 2)) for x in outs)


def solution(mesh):
    in_specs = (
        P("rep", None, "dom"),
        P("rep", None, "dom"),
        P("rep", None, "dom"),
        P("rep", "dom"),
        P("rep", "dom"),
        P("rep", "dom", None),
        P("rep", "dom"),
    ) + (P(),) * 10
    out_specs = (P("rep", None, "dom"), P("rep", None, "dom"), P("rep", None, "dom"))
    step = functools.partial(local, mesh.shape["dom"], mesh.shape["rep"])
    return jax.shard_map(step, mesh=mesh, in_specs=in_specs, out_specs=out_specs, check_vma=False)
```

```python
import functools
import math

import jax
import jax.numpy as jnp
from jax import lax
from jax.experimental import pallas as pl
from jax.experimental.pallas import tpu as pltpu
from jax.sharding import PartitionSpec as P

NB = 8
TILE = 128
NEI = 4

slab_width = 1.5
time_step = 0.5
basis_width = 0.3
norm_eps = 1e-06

f32 = jnp.float32
bf16 = jnp.bfloat16

LOG2E = math.log2(math.e)
SCALE = math.sqrt(LOG2E) / basis_width
TOP = 34.0
UNLIFT = 2.0**-TOP
STEEP = 4.0 * LOG2E
FAR = (40.0 * LOG2E) ** 2


def distinct(offsets, count):
    return list(dict.fromkeys(o % count for o in offsets))


def domain_sets(count):
    layer1 = distinct([0, -1, 1], count)
    layer0 = distinct(layer1 + [o + s for o in layer1 for s in (-1, 1)], count)
    held = distinct(layer0 + [o + s for o in layer0 for s in (-1, 1)], count)
    return layer1, layer0, held


def dot(a, b):
    return jnp.dot(a, b, preferred_element_type=f32)


def pack_kernel(loc, speed, push, kinds, ghosts, lists, counts, inertia, out):
    labels = kinds[...]
    mass = jnp.zeros(labels.shape, f32)
    for s in range(inertia.shape[0]):
        mass = jnp.where(labels == s, inertia[s], mass)
    inv_mass = 1.0 / mass
    atoms, tiles = labels.shape[1], counts.shape[1]
    out[...] = jnp.zeros(out.shape, f32)
    for d in range(3):
        out[d : d + 1, 0:atoms] = (
            loc[d] + time_step * speed[d] + 0.5 * time_step * time_step * push[d] * inv_mass
        )
        out[3 + d : 4 + d, 0:atoms] = speed[d] + 0.5 * time_step * push[d] * inv_mass
    out[6:7, 0:atoms] = labels.astype(f32)
    out[7:8, 0 : ghosts.shape[1]] = ghosts[...].astype(f32)
    out[0:NEI, atoms : atoms + tiles] = lists[0].astype(f32)
    out[NEI : NEI + 1, atoms : atoms + tiles] = counts[...].astype(f32)


def weights_kernel(
    kind, coef, gain, mix, target, source, swaps, levels, taper, inertia, wide, columns, small
):
    me = lax.axis_index("rep")
    lane = lax.broadcasted_iota(jnp.int32, (1, TILE), 1)
    factors, masses = jnp.zeros((1, TILE), f32), jnp.zeros((1, TILE), f32)
    for b in range(NB):
        scale = math.exp(-b * b) * UNLIFT / (math.sqrt(TILE * NEI * TILE) * SCALE)
        factors = jnp.where(lane == b, taper[b] * scale, factors)
    for s in range(inertia.shape[0]):
        masses = jnp.where(lane == s, inertia[s], masses)
    quotient = jnp.full((1, TILE), levels[me], f32) / jnp.full((1, TILE), levels[swaps[me]], f32)
    small[0:1] = factors
    small[1:2] = masses
    small[2:3] = jnp.sqrt(quotient)
    small[3:8] = jnp.zeros((5, TILE), f32)
    species = kind.shape[0]
    kinds_f = jnp.transpose(kind[...].astype(f32), (1, 0))
    coef_t = [jnp.transpose(coef[layer], (1, 0)) for layer in range(2)]
    u = []
    for b in range(NB):
        u.append(kinds_f * (coef_t[0][:, b : b + 1] * math.exp(-b * b)))
        columns[b] = jnp.broadcast_to(coef_t[1][:, b : b + 1] * math.exp(-b * b), columns.shape[1:])
    u = jnp.concatenate(u, axis=1)
    high = u.astype(bf16)
    wide[:, 0:TILE] = high
    wide[:, TILE : 2 * TILE] = (u - high.astype(f32)).astype(bf16)
    wide[:, 2 * TILE : 3 * TILE] = high
    gain_t = jnp.transpose(gain[...], (1, 0))
    for layer in range(2):
        columns[NB + layer] = jnp.broadcast_to(gain_t[:, layer : layer + 1], columns.shape[1:])
        wide[:, (3 + 2 * layer) * TILE : (4 + 2 * layer) * TILE] = jnp.transpose(
            mix[layer].astype(f32), (1, 0)
        ).astype(bf16)
    wide[:, 4 * TILE : 5 * TILE] = jnp.concatenate(
        [kinds_f, jnp.zeros((kinds_f.shape[0], TILE - species), f32)], axis=1
    ).astype(bf16)
    both = lax.dot_general(
        source[...], target[...], (((1,), (1,)), ((), ())), preferred_element_type=f32
    )
    high = both.astype(bf16)
    wide[:, 6 * TILE : 7 * TILE] = high
    wide[:, 7 * TILE : 8 * TILE] = (both - high.astype(f32)).astype(bf16)


def lanes_of(parts):
    return jnp.concatenate(parts, axis=1)


def activate(messages, gain):
    messages = messages * UNLIFT
    inverse = lax.rsqrt(jnp.mean(messages * messages, axis=0, keepdims=True) + norm_eps)
    v = messages * inverse * gain
    return (v / (1.0 + jnp.exp(-v))).astype(bf16)


def main_kernel(plan, *refs):
    count, atoms, ghost, species = plan
    layer1, layer0, held = domain_sets(count)
    tiles = atoms // TILE
    ghost_tiles = ghost // TILE
    ext_tiles = tiles + 2 * ghost_tiles
    n = len(held)
    outside = refs[: n + 3]
    outputs = refs[n + 3 : n + 6]
    held_data, wide, columns, small = refs[n + 6 : n + 10]
    pos_out, vel_out, force_out, arrivals, departures = refs[n + 10 : n + 15]
    data = {o: held_data.at[at] for at, o in enumerate(held)}
    inward = [
        pltpu.make_async_copy(src, dst, arrivals.at[at])
        for at, (src, dst) in enumerate(
            zip(outside, [held_data.at[at] for at in range(n)] + [wide, columns, small])
        )
    ]
    for c in inward:
        c.start()
    for c in inward[:n]:
        c.wait()
    (
        far_t,
        near_rhs,
        onehot,
        split_pos,
        species_sums,
        ghost_pick,
        hidden1,
        hidden2,
        ext_hidden,
        message_rows,
        envelopes,
        turned,
        asked,
        pulls,
        ints,
        sm,
        sem,
    ) = refs[n + 15 : -3]
    basis, squares = refs[-3], refs[-2:]
    u_parts = wide.at[:, 0 : 3 * TILE]
    mix_kind = wide.at[:, 3 * TILE : 4 * TILE + 16]
    mix_second = wide.at[:, 5 * TILE : 6 * TILE]
    both_parts = wide.at[:, 6 * TILE : 8 * TILE]
    kept = basis.shape[0]

    for at, o in enumerate(layer0):
        ints[at] = data[o][:, atoms : atoms + TILE].astype(jnp.int32)
    copies = [
        pltpu.make_async_copy(ints.at[at], sm.at[at], sem.at[at]) for at in range(len(layer0))
    ]
    for c in copies:
        c.start()

    outward = [
        pltpu.make_async_copy(src, dst, departures.at[at])
        for at, (src, dst) in enumerate(zip((pos_out, vel_out, force_out), outputs))
    ]
    for d in range(3):
        pos_out[d] = data[0][d : d + 1, 0:atoms]
    outward[0].start()

    row_id = lax.broadcasted_iota(jnp.int32, (8, TILE), 0)
    species_id = lax.broadcasted_iota(jnp.int32, (16, TILE), 0).astype(f32)
    def picked(o, first):
        src = data[o]
        idx = src[7:8, first : first + TILE].astype(jnp.int32)
        idx = jnp.broadcast_to(idx, (8, TILE))
        lane = idx & (TILE - 1)
        block = idx // TILE
        got = jnp.zeros((8, TILE), f32)
        for c in range(tiles):
            here = jnp.take_along_axis(
                src[:, c * TILE : (c + 1) * TILE], lane, axis=1, mode="promise_in_bounds"
            )
            got = jnp.where(block == c, here, got)
        return got

    def thirds(x):
        hi = x.astype(bf16).astype(f32)
        mid = (x - hi).astype(bf16).astype(f32)
        return hi, mid, x - hi - mid

    def rows_of(*rows):
        block = jnp.zeros((8, TILE), f32)
        for r, row in enumerate(rows):
            block = jnp.where(row_id == r, row, block)
        return block

    nowhere = rows_of(1e30, 0.0, 0.0, 1.0, 1.0, 1.0, 1.0)
    blank = jnp.zeros((8, TILE), f32)
    for at in range(len(layer0)):
        far_t[at, ext_tiles] = jnp.transpose(
            jnp.concatenate([blank] * 6 + [nowhere, rows_of(1e30)], axis=0), (1, 0)
        ).astype(bf16)

    for at, o in enumerate(layer0):
        lower, upper = (o - 1) % count, (o + 1) % count
        for e in range(ext_tiles):
            if e < tiles:
                block, shift = data[o][:, e * TILE : (e + 1) * TILE], 0.0
            elif e < tiles + ghost_tiles:
                block, shift = picked(lower, ghost + (e - tiles) * TILE), -slab_width
            else:
                block, shift = picked(upper, (e - tiles - ghost_tiles) * TILE), slab_width
            moved = jnp.where(row_id == 0, block + shift, block) - 0.5 * slab_width
            moved = jnp.where(row_id < 3, moved * SCALE, 0.0)
            onehot[at, e] = jnp.where(species_id == block[6:7, :], 1.0, 0.0).astype(bf16)
            hi, mid, low = thirds(moved)
            size = jnp.sum(moved * moved, axis=0, keepdims=True)
            sizes, steep_sizes = thirds(size), thirds(size * STEEP)
            far_t[at, e] = jnp.transpose(
                jnp.concatenate(
                    [hi, hi, hi, mid, mid, low]
                    + [rows_of(*sizes, 1.0, 1.0, 1.0, 1.0), rows_of(*steep_sizes)],
                    axis=0,
                ),
                (1, 0),
            ).astype(bf16)
            if o == 0:
                split_pos[e] = jnp.concatenate([hi, mid, low, rows_of(1.0)], axis=0).astype(bf16)
            if e < tiles:
                first, second, third = thirds(moved * -2.0)
                power = [-first, -second, -third, -first, -second, -first]
                power += [rows_of(-1.0, -1.0, -1.0, *[-x for x in sizes], TOP), blank]
                first, second, third = thirds(moved * (-2.0 * STEEP))
                steep = [first, second, third, first, second, first]
                steep += [rows_of(0.0, 0.0, 0.0, *steep_sizes), rows_of(1.0, 1.0, 1.0)]
                near_rhs[at, e] = lanes_of(
                    [jnp.concatenate(power, axis=0), jnp.concatenate(steep, axis=0)]
                ).astype(bf16)

    for c in copies:
        c.wait()

    def offsets(at, t):
        far = [
            far_t[at, jnp.where(k < sm[at, NEI, t], sm[at, k, t], ext_tiles)] for k in range(NEI)
        ]
        return dot(jnp.concatenate(far, axis=0), near_rhs[at, t])

    def basis_step(at, t, values):
        own = at == 0
        place = min(at, kept - 1)
        sums = [None] * (NB // 2)
        for half in range(NEI // 2):
            rows = slice(2 * half * TILE, 2 * (half + 1) * TILE)
            lhs = lanes_of([onehot[at, sm[at, 2 * half + k, t]] for k in range(2)])
            power = values[rows, 0:TILE]
            square = jnp.minimum(jnp.maximum(values[rows, TILE : 2 * TILE], 1e-30), FAR)
            slope = square * lax.rsqrt(square)
            ratio = jnp.exp2(slope)
            step = slope + slope
            envelope = None
            for p in range(NB // 2):
                even = jnp.exp2(power)
                odd = even * ratio
                pair = lanes_of([even.astype(bf16), odd.astype(bf16)])
                basis[place, t, rows, 2 * p * TILE : 2 * (p + 1) * TILE] = pair
                part = dot(lhs, pair)
                sums[p] = part if half == 0 else sums[p] + part
                if own:
                    part = even * small[0, 2 * p] + odd * small[0, 2 * p + 1]
                    envelope = part if p == 0 else envelope + part
                if p < NB // 2 - 1:
                    power = power + step
            if own:
                envelopes[t, rows] = envelope
        sums = [x[:, k * TILE : (k + 1) * TILE] for x in sums for k in range(2)]
        sums = jnp.concatenate(sums, axis=0)
        high = sums.astype(bf16)
        low = (sums - high.astype(f32)).astype(bf16)
        species_sums[at, t] = jnp.concatenate([high, high, low], axis=0)

    def first_layer(at):
        messages = dot(u_parts[...], lanes_of([species_sums[at, t] for t in range(tiles)]))
        activations = [
            activate(messages[:, t * TILE : (t + 1) * TILE], columns[NB]) for t in range(tiles)
        ]
        kinds = lanes_of([onehot[at, t] for t in range(tiles)])
        hidden = dot(mix_kind[...], jnp.concatenate([lanes_of(activations), kinds], axis=0))
        for t in range(tiles):
            block = hidden[:, t * TILE : (t + 1) * TILE].astype(bf16)
            hidden1[at, t] = block
            if at < len(layer1):
                ext_hidden[at, t] = block

    def pick_step(at, c):
        chosen = data[layer0[at]][7:8, 0 : 2 * ghost]
        rows = lax.broadcasted_iota(jnp.int32, (TILE, 2 * ghost), 0) + c * TILE
        ghost_pick[at, c * TILE : (c + 1) * TILE, :] = jnp.where(
            rows.astype(f32) == chosen, 1.0, 0.0
        ).astype(bf16)

    def extend(target, source_hidden, sets, o):
        for side, other in ((0, (o - 1) % count), (1, (o + 1) % count)):
            at = sets.index(other)
            rows = lanes_of([source_hidden[at, t] for t in range(tiles)])
            first = ghost if side == 0 else 0
            got = dot(
                rows, ghost_pick[layer0.index(other), :, first : first + ghost]
            ).astype(bf16)
            for g in range(ghost_tiles):
                target[tiles + side * ghost_tiles + g] = got[:, g * TILE : (g + 1) * TILE]

    def second_step(keep, t):
        at = layer0.index(layer1[keep])
        lhs = lanes_of([ext_hidden[keep, sm[at, k, t]] for k in range(NEI)])
        sums = dot(lhs, basis[keep, t])
        messages = None
        for b in range(NB):
            part = sums[:, b * TILE : (b + 1) * TILE] * columns[b]
            messages = part if messages is None else messages + part
        message_rows[keep, t] = messages

    def finish_second(keep, activations):
        at = layer0.index(layer1[keep])
        added = dot(mix_second[...], lanes_of(activations))
        for t in range(tiles):
            block = hidden1[at, t].astype(f32) + added[:, t * TILE : (t + 1) * TILE]
            hidden2[keep, t] = block.astype(bf16)

    def turn(block):
        return jnp.transpose(block.astype(f32), (1, 0)).astype(bf16)

    def import_final():
        extend(last, hidden2, layer1, 0)
        for e in range(tiles, ext_tiles):
            turned[e] = turn(last[e])

    last = ext_hidden.at[len(layer1)]
    order = list(range(1, len(layer1))) + [0]
    jobs = [
        functools.partial(pick_step, at, c) for at in range(len(layer0)) for c in range(tiles)
    ]
    imports = {
        keep: functools.partial(extend, ext_hidden.at[keep], hidden1, layer0, o)
        for keep, o in enumerate(layer1)
    }
    import_of = dict(imports)
    ready = set()

    def close_first(at):
        first_layer(at)
        ready.add(layer0[at])
        for keep, o in enumerate(layer1):
            if keep in imports and {(o - 1) % count, (o + 1) % count} <= ready:
                jobs.append(imports.pop(keep))

    for c in inward[n:]:
        c.wait()
    sequence = [(at, t) for at in range(len(layer0)) for t in range(tiles)]
    squares[0][...] = offsets(0, 0)
    for i, (at, t) in enumerate(sequence):
        if i + 1 < len(sequence):
            upcoming = offsets(*sequence[i + 1])
        basis_step(at, t, squares[i % 2])
        if i + 1 < len(sequence):
            squares[(i + 1) % 2][...] = upcoming
        if at:
            for _ in range(min(len(jobs), 4)):
                jobs.pop(0)()
        if t == tiles - 1 and at < len(layer0) - 1:
            jobs.insert(0, functools.partial(close_first, at))
    for job in jobs:
        job()
    jobs = []
    close_first(len(layer0) - 1)
    if import_of[order[0]] in jobs:
        jobs.remove(import_of[order[0]])
        import_of[order[0]]()
    pending = list(jobs)

    for keep in order:
        activations = []
        for t in range(tiles):
            second_step(keep, t)
            if t:
                activations.append(activate(message_rows[keep, t - 1], columns[NB + 1]))
            if pending and t % 2:
                pending.pop(0)()
        activations.append(activate(message_rows[keep, tiles - 1], columns[NB + 1]))
        for job in pending:
            job()
        pending = [functools.partial(finish_second, keep, activations)]
        if keep and keep == order[-2]:
            pending.append(import_final)
    for job in pending:
        job()
    if len(order) == 1:
        import_final()
    own_hidden = [hidden2[0, t] for t in range(tiles)]
    for t in range(tiles):
        turned[t] = turn(own_hidden[t])
    own_hidden = lanes_of(own_hidden)
    wanted = dot(both_parts[...], jnp.concatenate([own_hidden, own_hidden], axis=0)).astype(bf16)
    empty = jnp.zeros((TILE, TILE), bf16)
    duos = range(tiles // 2)
    for q in duos:
        first, second = (wanted[:, t * TILE : (t + 1) * TILE] for t in (2 * q, 2 * q + 1))
        asked[q] = jnp.concatenate([lanes_of([first, empty]), lanes_of([empty, second])], axis=0)

    def weigh(q):
        lhs = [lanes_of([turned[sm[0, k, t]] for t in (2 * q, 2 * q + 1)]) for k in range(NEI)]
        scores = dot(jnp.concatenate(lhs, axis=0), asked[q])
        return (scores * lanes_of([envelopes[t] for t in (2 * q, 2 * q + 1)])).astype(bf16)

    def pull(q, weight):
        places = [
            lanes_of([split_pos[sm[0, k, t]] for k in range(NEI)]) for t in (2 * q, 2 * q + 1)
        ]
        got = dot(jnp.concatenate(places, axis=0), weight)
        for side in range(2):
            part = got[32 * side : 32 * (side + 1), side * TILE : (side + 1) * TILE]
            pulls[2 * q + side] = jnp.concatenate(
                [part[0:8] + part[8:16] + part[16:24], part[24:32]], axis=0
            )

    weights = {0: weigh(0)}
    for q in duos:
        if q + 1 in duos:
            weights[q + 1] = weigh(q + 1)
        pull(q, weights.pop(q))

    own = data[0]
    labels = own[6:7, 0:atoms]
    mass = jnp.zeros(labels.shape, f32)
    for s in range(species):
        mass = jnp.where(labels == s, small[1, s], mass)
    inv_mass = 1.0 / mass
    for t in range(tiles):
        lanes = slice(t * TILE, (t + 1) * TILE)
        got = pulls[t]
        force = got[0:8] - (own[:, lanes] - 0.5 * slab_width) * SCALE * got[8:9]
        velocity = own[3:6, lanes] + 0.5 * time_step * force[0:3] * inv_mass[:, lanes]
        velocity = velocity * small[2, 0]
        for d in range(3):
            force_out[d, :, lanes] = force[d : d + 1]
            vel_out[d, :, lanes] = velocity[d : d + 1]
    for c in outward[1:]:
        c.start()
    for c in outward:
        c.wait()


def local(
    count,
    replicas,
    particle_locations,
    particle_speeds,
    current_pushes,
    particle_kinds,
    halo_particle_labels,
    adjacent_block_labels,
    adjacent_place_totals,
    kind_vectors,
    kind_inertia,
    stepwise_distance_coefficients,
    signal_scaling_factors,
    feature_blend_coefficients,
    target_projection_array,
    source_projection_array,
    push_distance_taper,
    thermal_levels,
    granted_swaps,
):
    atoms = particle_locations.shape[2]
    ghost = halo_particle_labels.shape[1] // 2
    channels = kind_vectors.shape[1]
    tiles = atoms // TILE
    ext_tiles = tiles + 2 * (ghost // TILE)
    layer1, layer0, held = domain_sets(count)
    vmem = pl.BlockSpec(memory_space=pltpu.VMEM)
    smem = pl.BlockSpec(memory_space=pltpu.SMEM)
    shape = jax.ShapeDtypeStruct

    packed = pl.pallas_call(
        pack_kernel,
        out_shape=shape((8, atoms + TILE), f32),
        in_specs=[vmem] * 7 + [smem],
        out_specs=vmem,
    )(
        jnp.transpose(particle_locations, (1, 0, 2)),
        jnp.transpose(particle_speeds, (1, 0, 2)),
        jnp.transpose(current_pushes, (1, 0, 2)),
        particle_kinds,
        halo_particle_labels,
        jnp.transpose(adjacent_block_labels, (0, 2, 1)),
        adjacent_place_totals,
        kind_inertia,
    )

    even = [(i, i ^ 1) for i in range(replicas)]
    odd = [(i, ((i + 1) ^ 1) - 1) for i in range(1, replicas - 1)]
    odd_all = [(a * count + d, b * count + d) for a, b in odd for d in range(count)] + [
        (r * count + d, r * count + (d + 1) % count) for r in (0, replicas - 1) for d in range(count)
    ]
    from_even = lax.ppermute(packed, "rep", even)
    from_odd = lax.ppermute(packed, ("rep", "dom"), odd_all)
    me = lax.axis_index("rep")
    partner = granted_swaps[me]
    low = jnp.minimum(me, partner)
    chosen = jnp.where(partner == me, packed, jnp.where(low % 2 == 0, from_even, from_odd))
    data = [
        chosen
        if o == 0
        else lax.ppermute(chosen, "dom", [((d + o) % count, d) for d in range(count)])
        for o in held
    ]

    weights = pl.pallas_call(
        weights_kernel,
        out_shape=[
            shape((channels, 8 * TILE), bf16),
            shape((NB + 2, channels, TILE), f32),
            shape((8, TILE), f32),
        ],
        in_specs=[vmem] * 6 + [smem] * 4,
        out_specs=[vmem] * 3,
        compiler_params=pltpu.CompilerParams(vmem_limit_bytes=8 * 2**20),
        cost_estimate=pl.CostEstimate(flops=10**6, bytes_accessed=10**6, transcendentals=0),
    )(
        kind_vectors,
        stepwise_distance_coefficients,
        signal_scaling_factors,
        feature_blend_coefficients,
        target_projection_array,
        source_projection_array,
        granted_swaps,
        thermal_levels,
        push_distance_taper,
        kind_inertia,
    )

    n0, n1 = len(layer0), len(layer1)
    kept = (n1 + (n0 > n1), tiles, NEI * TILE, NB * TILE)
    buffers = [
        ((n0, ext_tiles + 1, TILE, 64), bf16),
        ((n0, tiles, 64, 2 * TILE), bf16),
        ((n0, ext_tiles, 16, TILE), bf16),
        ((ext_tiles, 32, TILE), bf16),
        ((n0, tiles, 3 * NB * 16, TILE), bf16),
        ((n0, atoms, 2 * ghost), bf16),
        ((n0, tiles, TILE, TILE), bf16),
        ((n1, tiles, TILE, TILE), bf16),
        ((n1 + 1, ext_tiles, TILE, TILE), bf16),
        ((n1, tiles, TILE, TILE), f32),
        ((tiles, NEI * TILE, TILE), f32),
        ((ext_tiles, TILE, TILE), bf16),
        ((tiles // 2, 2 * TILE, 2 * TILE), bf16),
        ((tiles, 16, TILE), f32),
        ((n0, 8, TILE), jnp.int32),
    ]
    inner = [
        ((len(held), 8, atoms + TILE), f32),
        ((channels, 8 * TILE), bf16),
        ((NB + 2, channels, TILE), f32),
    ]
    outgoing = [((3, 1, atoms), f32)] * 3
    outer = [(kept, bf16)] + [((NEI * TILE, 2 * TILE), f32)] * 2
    scratch = [pltpu.VMEM(*buffer) for buffer in inner] + [pltpu.SMEM((8, TILE), f32)]
    scratch += [pltpu.VMEM(*buffer) for buffer in outgoing]
    scratch += [pltpu.SemaphoreType.DMA((len(held) + 3,)), pltpu.SemaphoreType.DMA((3,))]
    scratch += [pltpu.VMEM(*buffer) for buffer in buffers] + [
        pltpu.SMEM((n0, 8, TILE), jnp.int32),
        pltpu.SemaphoreType.DMA((n0,)),
    ]
    scratch += [pltpu.VMEM(*buffer) for buffer in outer]
    limit = 9 * 2**20 + sum(
        math.prod(dims[:-1]) * max(dims[-1], TILE) * jnp.dtype(kind).itemsize
        for dims, kind in inner + outgoing + buffers + outer
    )

    outs = pl.pallas_call(
        functools.partial(main_kernel, (count, atoms, ghost, kind_vectors.shape[0])),
        out_shape=[shape((3, 1, atoms), f32)] * 3,
        in_specs=[pl.BlockSpec(memory_space=pl.ANY)] * (len(held) + 3),
        out_specs=[pl.BlockSpec(memory_space=pl.ANY)] * 3,
        scratch_shapes=scratch,
        compiler_params=pltpu.CompilerParams(vmem_limit_bytes=limit),
    )(
        *data,
        *weights,
    )
    return tuple(jnp.transpose(x, (1, 0, 2)) for x in outs)


def solution(mesh):
    in_specs = (
        P("rep", None, "dom"),
        P("rep", None, "dom"),
        P("rep", None, "dom"),
        P("rep", "dom"),
        P("rep", "dom"),
        P("rep", "dom", None),
        P("rep", "dom"),
    ) + (P(),) * 10
    out_specs = (P("rep", None, "dom"), P("rep", None, "dom"), P("rep", None, "dom"))
    step = functools.partial(local, mesh.shape["dom"], mesh.shape["rep"])
    return jax.shard_map(step, mesh=mesh, in_specs=in_specs, out_specs=out_specs, check_vma=False)
```

```python
import functools
import math

import jax
import jax.numpy as jnp
from jax import lax
from jax.experimental import pallas as pl
from jax.experimental.pallas import tpu as pltpu
from jax.sharding import PartitionSpec as P

NB = 8
TILE = 128
NEI = 4

slab_width = 1.5
time_step = 0.5
basis_width = 0.3
norm_eps = 1e-06

f32 = jnp.float32
bf16 = jnp.bfloat16

LOG2E = math.log2(math.e)
SCALE = math.sqrt(LOG2E) / basis_width
TOP = 34.0
UNLIFT = 2.0**-TOP
STEEP = 4.0 * LOG2E
FAR = (40.0 * LOG2E) ** 2


def distinct(offsets, count):
    return list(dict.fromkeys(o % count for o in offsets))


def domain_sets(count):
    layer1 = distinct([0, -1, 1], count)
    layer0 = distinct(layer1 + [o + s for o in layer1 for s in (-1, 1)], count)
    held = distinct(layer0 + [o + s for o in layer0 for s in (-1, 1)], count)
    return layer1, layer0, held


def dot(a, b):
    return jnp.dot(a, b, preferred_element_type=f32)


def pack_kernel(
    loc, speed, push, kinds, ghosts, lists, counts, inertia, swaps, levels, taper, out, small
):
    me = lax.axis_index("rep")
    lane = lax.broadcasted_iota(jnp.int32, (1, TILE), 1)
    factors, masses = jnp.zeros((1, TILE), f32), jnp.zeros((1, TILE), f32)
    for b in range(NB):
        scale = math.exp(-b * b) * UNLIFT / (math.sqrt(TILE * NEI * TILE) * SCALE)
        factors = jnp.where(lane == b, taper[b] * scale, factors)
    for s in range(inertia.shape[0]):
        masses = jnp.where(lane == s, inertia[s], masses)
    quotient = jnp.full((1, TILE), levels[me], f32) / jnp.full((1, TILE), levels[swaps[me]], f32)
    small[0:1] = factors
    small[1:2] = masses
    small[2:3] = jnp.sqrt(quotient)
    partner = swaps[me]
    rung = jnp.where(partner == me, 0, 1 + (jnp.minimum(me, partner) & 1))
    small[3:8] = jnp.full((5, TILE), rung, jnp.int32).astype(f32)
    labels = kinds[...]
    mass = jnp.zeros(labels.shape, f32)
    for s in range(inertia.shape[0]):
        mass = jnp.where(labels == s, inertia[s], mass)
    inv_mass = 1.0 / mass
    atoms, tiles = labels.shape[1], counts.shape[1]
    out[...] = jnp.zeros(out.shape, f32)
    for d in range(3):
        out[d : d + 1, 0:atoms] = (
            loc[d] + time_step * speed[d] + 0.5 * time_step * time_step * push[d] * inv_mass
        )
        out[3 + d : 4 + d, 0:atoms] = speed[d] + 0.5 * time_step * push[d] * inv_mass
    out[6:7, 0:atoms] = labels.astype(f32)
    out[7:8, 0 : ghosts.shape[1]] = ghosts[...].astype(f32)
    out[0:NEI, atoms : atoms + tiles] = lists[0].astype(f32)
    out[NEI : NEI + 1, atoms : atoms + tiles] = counts[...].astype(f32)


def weights_kernel(
    kind, coef, gain, mix, projections, wide, columns
):
    species = kind.shape[0]
    kinds_f = jnp.transpose(kind[...].astype(f32), (1, 0))
    coef_t = [jnp.transpose(coef[layer], (1, 0)) for layer in range(2)]
    u = []
    for b in range(NB):
        u.append(kinds_f * (coef_t[0][:, b : b + 1] * math.exp(-b * b)))
        columns[b] = jnp.broadcast_to(coef_t[1][:, b : b + 1] * math.exp(-b * b), columns.shape[1:])
    u = jnp.concatenate(u, axis=1)
    high = u.astype(bf16)
    wide[:, 0:TILE] = high
    wide[:, TILE : 2 * TILE] = (u - high.astype(f32)).astype(bf16)
    wide[:, 2 * TILE : 3 * TILE] = high
    gain_t = jnp.transpose(gain[...], (1, 0))
    for layer in range(2):
        columns[NB + layer] = jnp.broadcast_to(gain_t[:, layer : layer + 1], columns.shape[1:])
        wide[:, (3 + 2 * layer) * TILE : (4 + 2 * layer) * TILE] = jnp.transpose(
            mix[layer].astype(f32), (1, 0)
        ).astype(bf16)
    wide[:, 4 * TILE : 5 * TILE] = jnp.concatenate(
        [kinds_f, jnp.zeros((kinds_f.shape[0], TILE - species), f32)], axis=1
    ).astype(bf16)
    both = projections[...]
    high = both.astype(bf16)
    wide[:, 6 * TILE : 7 * TILE] = high
    wide[:, 7 * TILE : 8 * TILE] = (both - high.astype(f32)).astype(bf16)


def lanes_of(parts):
    return jnp.concatenate(parts, axis=1)


def activate(messages, gain):
    messages = messages * UNLIFT
    inverse = lax.rsqrt(jnp.mean(messages * messages, axis=0, keepdims=True) + norm_eps)
    v = messages * inverse * gain
    return (v / (1.0 + jnp.exp(-v))).astype(bf16)


def main_kernel(plan, *refs):
    count, atoms, ghost, species = plan
    layer1, layer0, held = domain_sets(count)
    tiles = atoms // TILE
    ghost_tiles = ghost // TILE
    ext_tiles = tiles + 2 * ghost_tiles
    n = len(held)
    offers = refs[: 3 * n]
    tables = refs[3 * n : 3 * n + 3]
    refs = refs[3 * n + 3 :]
    outputs = refs[:3]
    offered, held_data, rung, wide, columns, small = refs[3:9]
    pos_out, vel_out, force_out, arrivals, departures = refs[9:14]
    data = {o: held_data.at[at] for at, o in enumerate(held)}
    inward = [
        pltpu.make_async_copy(src, dst, arrivals.at[at])
        for at, (src, dst) in enumerate(
            zip(
                (*offers, tables[2], *tables),
                [offered.at[at] for at in range(3 * n)] + [rung, wide, columns, small],
            )
        )
    ]
    for c in inward:
        c.start()
    for c in inward[: 3 * n + 1]:
        c.wait()
    place = rung[3:4]
    for at in range(n):
        for first in range(0, atoms + TILE, TILE):
            lanes = slice(first, first + TILE)
            here, even, odd = (offered[3 * at + k, :, lanes] for k in range(3))
            held_data[at, :, lanes] = jnp.where(place == 0.0, here, jnp.where(place == 1.0, even, odd))

    (
        far_t,
        near_rhs,
        onehot,
        split_pos,
        species_sums,
        ghost_pick,
        hidden1,
        hidden2,
        ext_hidden,
        message_rows,
        envelopes,
        turned,
        asked,
        pulls,
        ints,
        sm,
        sem,
    ) = refs[14:-3]
    basis, squares = refs[-3], refs[-2:]
    u_parts = wide.at[:, 0 : 3 * TILE]
    mix_kind = wide.at[:, 3 * TILE : 4 * TILE + 16]
    mix_second = wide.at[:, 5 * TILE : 6 * TILE]
    both_parts = wide.at[:, 6 * TILE : 8 * TILE]
    kept = basis.shape[0]

    for at, o in enumerate(layer0):
        ints[at] = data[o][:, atoms : atoms + TILE].astype(jnp.int32)
    copies = [
        pltpu.make_async_copy(ints.at[at], sm.at[at], sem.at[at]) for at in range(len(layer0))
    ]
    for c in copies:
        c.start()

    outward = [
        pltpu.make_async_copy(src, dst, departures.at[at])
        for at, (src, dst) in enumerate(zip((pos_out, vel_out, force_out), outputs))
    ]
    for d in range(3):
        pos_out[d] = data[0][d : d + 1, 0:atoms]
    outward[0].start()

    row_id = lax.broadcasted_iota(jnp.int32, (8, TILE), 0)
    species_id = lax.broadcasted_iota(jnp.int32, (16, TILE), 0).astype(f32)
    def picked(o, first):
        src = data[o]
        idx = src[7:8, first : first + TILE].astype(jnp.int32)
        idx = jnp.broadcast_to(idx, (8, TILE))
        lane = idx & (TILE - 1)
        block = idx // TILE
        got = jnp.zeros((8, TILE), f32)
        for c in range(tiles):
            here = jnp.take_along_axis(
                src[:, c * TILE : (c + 1) * TILE], lane, axis=1, mode="promise_in_bounds"
            )
            got = jnp.where(block == c, here, got)
        return got

    def thirds(x):
        hi = x.astype(bf16).astype(f32)
        mid = (x - hi).astype(bf16).astype(f32)
        return hi, mid, x - hi - mid

    def rows_of(*rows):
        block = jnp.zeros((8, TILE), f32)
        for r, row in enumerate(rows):
            block = jnp.where(row_id == r, row, block)
        return block

    nowhere = rows_of(1e30, 0.0, 0.0, 1.0, 1.0, 1.0, 1.0)
    blank = jnp.zeros((8, TILE), f32)
    for at in range(len(layer0)):
        far_t[at, ext_tiles] = jnp.transpose(
            jnp.concatenate([blank] * 6 + [nowhere, rows_of(1e30)], axis=0), (1, 0)
        ).astype(bf16)

    for at, o in enumerate(layer0):
        lower, upper = (o - 1) % count, (o + 1) % count
        for e in range(ext_tiles):
            if e < tiles:
                block, shift = data[o][:, e * TILE : (e + 1) * TILE], 0.0
            elif e < tiles + ghost_tiles:
                block, shift = picked(lower, ghost + (e - tiles) * TILE), -slab_width
            else:
                block, shift = picked(upper, (e - tiles - ghost_tiles) * TILE), slab_width
            moved = jnp.where(row_id == 0, block + shift, block) - 0.5 * slab_width
            moved = jnp.where(row_id < 3, moved * SCALE, 0.0)
            onehot[at, e] = jnp.where(species_id == block[6:7, :], 1.0, 0.0).astype(bf16)
            hi, mid, low = thirds(moved)
            size = jnp.sum(moved * moved, axis=0, keepdims=True)
            sizes, steep_sizes = thirds(size), thirds(size * STEEP)
            far_t[at, e] = jnp.transpose(
                jnp.concatenate(
                    [hi, hi, hi, mid, mid, low]
                    + [rows_of(*sizes, 1.0, 1.0, 1.0, 1.0), rows_of(*steep_sizes)],
                    axis=0,
                ),
                (1, 0),
            ).astype(bf16)
            if o == 0:
                split_pos[e] = jnp.concatenate([hi, mid, low, rows_of(1.0)], axis=0).astype(bf16)
            if e < tiles:
                first, second, third = thirds(moved * -2.0)
                power = [-first, -second, -third, -first, -second, -first]
                power += [rows_of(-1.0, -1.0, -1.0, *[-x for x in sizes], TOP), blank]
                first, second, third = thirds(moved * (-2.0 * STEEP))
                steep = [first, second, third, first, second, first]
                steep += [rows_of(0.0, 0.0, 0.0, *steep_sizes), rows_of(1.0, 1.0, 1.0)]
                near_rhs[at, e] = lanes_of(
                    [jnp.concatenate(power, axis=0), jnp.concatenate(steep, axis=0)]
                ).astype(bf16)

    for c in copies:
        c.wait()

    def offsets(at, t):
        far = [
            far_t[at, jnp.where(k < sm[at, NEI, t], sm[at, k, t], ext_tiles)] for k in range(NEI)
        ]
        return dot(jnp.concatenate(far, axis=0), near_rhs[at, t])

    def basis_step(at, t, values):
        own = at == 0
        place = min(at, kept - 1)
        sums = [None] * (NB // 2)
        for half in range(NEI // 2):
            rows = slice(2 * half * TILE, 2 * (half + 1) * TILE)
            lhs = lanes_of([onehot[at, sm[at, 2 * half + k, t]] for k in range(2)])
            power = values[rows, 0:TILE]
            square = jnp.minimum(jnp.maximum(values[rows, TILE : 2 * TILE], 1e-30), FAR)
            slope = square * lax.rsqrt(square)
            ratio = jnp.exp2(slope)
            step = slope + slope
            envelope = None
            for p in range(NB // 2):
                even = jnp.exp2(power)
                odd = even * ratio
                pair = lanes_of([even.astype(bf16), odd.astype(bf16)])
                basis[place, t, rows, 2 * p * TILE : 2 * (p + 1) * TILE] = pair
                part = dot(lhs, pair)
                sums[p] = part if half == 0 else sums[p] + part
                if own:
                    part = even * small[0, 2 * p] + odd * small[0, 2 * p + 1]
                    envelope = part if p == 0 else envelope + part
                if p < NB // 2 - 1:
                    power = power + step
            if own:
                envelopes[t, rows] = envelope
        sums = [x[:, k * TILE : (k + 1) * TILE] for x in sums for k in range(2)]
        sums = jnp.concatenate(sums, axis=0)
        high = sums.astype(bf16)
        low = (sums - high.astype(f32)).astype(bf16)
        species_sums[at, t] = jnp.concatenate([high, high, low], axis=0)

    def first_layer(at):
        messages = dot(u_parts[...], lanes_of([species_sums[at, t] for t in range(tiles)]))
        activations = [
            activate(messages[:, t * TILE : (t + 1) * TILE], columns[NB]) for t in range(tiles)
        ]
        kinds = lanes_of([onehot[at, t] for t in range(tiles)])
        hidden = dot(mix_kind[...], jnp.concatenate([lanes_of(activations), kinds], axis=0))
        for t in range(tiles):
            block = hidden[:, t * TILE : (t + 1) * TILE].astype(bf16)
            hidden1[at, t] = block
            if at < len(layer1):
                ext_hidden[at, t] = block

    def pick_step(at, c):
        chosen = data[layer0[at]][7:8, 0 : 2 * ghost]
        rows = lax.broadcasted_iota(jnp.int32, (TILE, 2 * ghost), 0) + c * TILE
        ghost_pick[at, c * TILE : (c + 1) * TILE, :] = jnp.where(
            rows.astype(f32) == chosen, 1.0, 0.0
        ).astype(bf16)

    def extend(target, source_hidden, sets, o):
        for side, other in ((0, (o - 1) % count), (1, (o + 1) % count)):
            at = sets.index(other)
            rows = lanes_of([source_hidden[at, t] for t in range(tiles)])
            first = ghost if side == 0 else 0
            got = dot(
                rows, ghost_pick[layer0.index(other), :, first : first + ghost]
            ).astype(bf16)
            for g in range(ghost_tiles):
                target[tiles + side * ghost_tiles + g] = got[:, g * TILE : (g + 1) * TILE]

    def second_step(keep, t):
        at = layer0.index(layer1[keep])
        lhs = lanes_of([ext_hidden[keep, sm[at, k, t]] for k in range(NEI)])
        sums = dot(lhs, basis[keep, t])
        messages = None
        for b in range(NB):
            part = sums[:, b * TILE : (b + 1) * TILE] * columns[b]
            messages = part if messages is None else messages + part
        message_rows[keep, t] = messages

    def finish_second(keep, activations):
        at = layer0.index(layer1[keep])
        added = dot(mix_second[...], lanes_of(activations))
        for t in range(tiles):
            block = hidden1[at, t].astype(f32) + added[:, t * TILE : (t + 1) * TILE]
            hidden2[keep, t] = block.astype(bf16)

    def turn(block):
        return jnp.transpose(block.astype(f32), (1, 0)).astype(bf16)

    def import_final():
        extend(last, hidden2, layer1, 0)
        for e in range(tiles, ext_tiles):
            turned[e] = turn(last[e])

    last = ext_hidden.at[len(layer1)]
    order = list(range(1, len(layer1))) + [0]
    jobs = [
        functools.partial(pick_step, at, c) for at in range(len(layer0)) for c in range(tiles)
    ]
    imports = {
        keep: functools.partial(extend, ext_hidden.at[keep], hidden1, layer0, o)
        for keep, o in enumerate(layer1)
    }
    import_of = dict(imports)
    ready = set()

    def close_first(at):
        first_layer(at)
        ready.add(layer0[at])
        for keep, o in enumerate(layer1):
            if keep in imports and {(o - 1) % count, (o + 1) % count} <= ready:
                jobs.append(imports.pop(keep))

    for c in inward[3 * n + 1 :]:
        c.wait()
    sequence = [(at, t) for at in range(len(layer0)) for t in range(tiles)]
    squares[0][...] = offsets(0, 0)
    for i, (at, t) in enumerate(sequence):
        if i + 1 < len(sequence):
            upcoming = offsets(*sequence[i + 1])
        basis_step(at, t, squares[i % 2])
        if i + 1 < len(sequence):
            squares[(i + 1) % 2][...] = upcoming
        if at:
            for _ in range(min(len(jobs), 4)):
                jobs.pop(0)()
        if t == tiles - 1 and at < len(layer0) - 1:
            jobs.insert(0, functools.partial(close_first, at))
    for job in jobs:
        job()
    jobs = []
    close_first(len(layer0) - 1)
    if import_of[order[0]] in jobs:
        jobs.remove(import_of[order[0]])
        import_of[order[0]]()
    pending = list(jobs)

    for keep in order:
        activations = []
        for t in range(tiles):
            second_step(keep, t)
            if t:
                activations.append(activate(message_rows[keep, t - 1], columns[NB + 1]))
            if pending and t % 2:
                pending.pop(0)()
        activations.append(activate(message_rows[keep, tiles - 1], columns[NB + 1]))
        for job in pending:
            job()
        pending = [functools.partial(finish_second, keep, activations)]
        if keep and keep == order[-2]:
            pending.append(import_final)
    for job in pending:
        job()
    if len(order) == 1:
        import_final()
    own_hidden = [hidden2[0, t] for t in range(tiles)]
    for t in range(tiles):
        turned[t] = turn(own_hidden[t])
    own_hidden = lanes_of(own_hidden)
    wanted = dot(both_parts[...], jnp.concatenate([own_hidden, own_hidden], axis=0)).astype(bf16)
    empty = jnp.zeros((TILE, TILE), bf16)
    duos = range(tiles // 2)
    for q in duos:
        first, second = (wanted[:, t * TILE : (t + 1) * TILE] for t in (2 * q, 2 * q + 1))
        asked[q] = jnp.concatenate([lanes_of([first, empty]), lanes_of([empty, second])], axis=0)

    def weigh(q):
        lhs = [lanes_of([turned[sm[0, k, t]] for t in (2 * q, 2 * q + 1)]) for k in range(NEI)]
        scores = dot(jnp.concatenate(lhs, axis=0), asked[q])
        return (scores * lanes_of([envelopes[t] for t in (2 * q, 2 * q + 1)])).astype(bf16)

    def pull(q, weight):
        places = [
            lanes_of([split_pos[sm[0, k, t]] for k in range(NEI)]) for t in (2 * q, 2 * q + 1)
        ]
        got = dot(jnp.concatenate(places, axis=0), weight)
        for side in range(2):
            part = got[32 * side : 32 * (side + 1), side * TILE : (side + 1) * TILE]
            pulls[2 * q + side] = jnp.concatenate(
                [part[0:8] + part[8:16] + part[16:24], part[24:32]], axis=0
            )

    weights = {0: weigh(0)}
    for q in duos:
        if q + 1 in duos:
            weights[q + 1] = weigh(q + 1)
        pull(q, weights.pop(q))

    own = data[0]
    labels = own[6:7, 0:atoms]
    mass = jnp.zeros(labels.shape, f32)
    for s in range(species):
        mass = jnp.where(labels == s, small[1, s], mass)
    inv_mass = 1.0 / mass
    for t in range(tiles):
        lanes = slice(t * TILE, (t + 1) * TILE)
        got = pulls[t]
        force = got[0:8] - (own[:, lanes] - 0.5 * slab_width) * SCALE * got[8:9]
        velocity = own[3:6, lanes] + 0.5 * time_step * force[0:3] * inv_mass[:, lanes]
        velocity = velocity * small[2, 0]
        for d in range(3):
            force_out[d, :, lanes] = force[d : d + 1]
            vel_out[d, :, lanes] = velocity[d : d + 1]
    for c in outward[1:]:
        c.start()
    for c in outward:
        c.wait()


def local(
    count,
    replicas,
    particle_locations,
    particle_speeds,
    current_pushes,
    particle_kinds,
    halo_particle_labels,
    adjacent_block_labels,
    adjacent_place_totals,
    kind_vectors,
    kind_inertia,
    stepwise_distance_coefficients,
    signal_scaling_factors,
    feature_blend_coefficients,
    target_projection_array,
    source_projection_array,
    push_distance_taper,
    thermal_levels,
    granted_swaps,
):
    atoms = particle_locations.shape[2]
    ghost = halo_particle_labels.shape[1] // 2
    channels = kind_vectors.shape[1]
    tiles = atoms // TILE
    ext_tiles = tiles + 2 * (ghost // TILE)
    layer1, layer0, held = domain_sets(count)
    vmem = pl.BlockSpec(memory_space=pltpu.VMEM)
    smem = pl.BlockSpec(memory_space=pltpu.SMEM)
    shape = jax.ShapeDtypeStruct

    packed, small = pl.pallas_call(
        pack_kernel,
        out_shape=[shape((8, atoms + TILE), f32), shape((8, TILE), f32)],
        in_specs=[vmem] * 7 + [smem] * 4,
        out_specs=[vmem] * 2,
    )(
        jnp.transpose(particle_locations, (1, 0, 2)),
        jnp.transpose(particle_speeds, (1, 0, 2)),
        jnp.transpose(current_pushes, (1, 0, 2)),
        particle_kinds,
        halo_particle_labels,
        jnp.transpose(adjacent_block_labels, (0, 2, 1)),
        adjacent_place_totals,
        kind_inertia,
        granted_swaps,
        thermal_levels,
        push_distance_taper,
    )

    even = [(i, i ^ 1) for i in range(replicas)]
    odd = [(i, ((i + 1) ^ 1) - 1) for i in range(1, replicas - 1)]
    rim = [
        (r * count + d, r * count + (d + 1) % count) for r in (0, replicas - 1) for d in range(count)
    ]
    offers = []
    for o in held:
        beside = [((d + o) % count, d) for d in range(count)]
        here = packed if o == 0 else lax.ppermute(packed, "dom", beside)
        across = [(a * count + c, b * count + d) for a, b in odd for c, d in beside]
        offers += [
            here,
            lax.ppermute(here, "rep", even),
            lax.ppermute(packed, ("rep", "dom"), across + rim),
        ]
    projections = dot(source_projection_array, target_projection_array.T)
    weights = pl.pallas_call(
        weights_kernel,
        out_shape=[
            shape((channels, 8 * TILE), bf16),
            shape((NB + 2, channels, TILE), f32),
        ],
        in_specs=[vmem] * 5,
        out_specs=[vmem] * 2,
        compiler_params=pltpu.CompilerParams(vmem_limit_bytes=8 * 2**20),
        cost_estimate=pl.CostEstimate(flops=10**6, bytes_accessed=10**6, transcendentals=0),
    )(
        kind_vectors,
        stepwise_distance_coefficients,
        signal_scaling_factors,
        feature_blend_coefficients,
        projections,
    )

    n0, n1 = len(layer0), len(layer1)
    kept = (n1 + (n0 > n1), tiles, NEI * TILE, NB * TILE)
    buffers = [
        ((n0, ext_tiles + 1, TILE, 64), bf16),
        ((n0, tiles, 64, 2 * TILE), bf16),
        ((n0, ext_tiles, 16, TILE), bf16),
        ((ext_tiles, 32, TILE), bf16),
        ((n0, tiles, 3 * NB * 16, TILE), bf16),
        ((n0, atoms, 2 * ghost), bf16),
        ((n0, tiles, TILE, TILE), bf16),
        ((n1, tiles, TILE, TILE), bf16),
        ((n1 + 1, ext_tiles, TILE, TILE), bf16),
        ((n1, tiles, TILE, TILE), f32),
        ((tiles, NEI * TILE, TILE), f32),
        ((ext_tiles, TILE, TILE), bf16),
        ((tiles // 2, 2 * TILE, 2 * TILE), bf16),
        ((tiles, 16, TILE), f32),
        ((n0, 8, TILE), jnp.int32),
    ]
    inner = [
        ((3 * len(held), 8, atoms + TILE), f32),
        ((len(held), 8, atoms + TILE), f32),
        ((8, TILE), f32),
        ((channels, 8 * TILE), bf16),
        ((NB + 2, channels, TILE), f32),
    ]
    outgoing = [((3, 1, atoms), f32)] * 3
    outer = [(kept, bf16)] + [((NEI * TILE, 2 * TILE), f32)] * 2
    scratch = [pltpu.VMEM(*buffer) for buffer in inner] + [pltpu.SMEM((8, TILE), f32)]
    scratch += [pltpu.VMEM(*buffer) for buffer in outgoing]
    scratch += [pltpu.SemaphoreType.DMA((3 * len(held) + 4,)), pltpu.SemaphoreType.DMA((3,))]
    scratch += [pltpu.VMEM(*buffer) for buffer in buffers] + [
        pltpu.SMEM((n0, 8, TILE), jnp.int32),
        pltpu.SemaphoreType.DMA((n0,)),
    ]
    scratch += [pltpu.VMEM(*buffer) for buffer in outer]
    limit = 9 * 2**20 + sum(
        math.prod(dims[:-1]) * max(dims[-1], TILE) * jnp.dtype(kind).itemsize
        for dims, kind in inner + outgoing + buffers + outer
    )

    outs = pl.pallas_call(
        functools.partial(main_kernel, (count, atoms, ghost, kind_vectors.shape[0])),
        out_shape=[shape((3, 1, atoms), f32)] * 3,
        in_specs=[pl.BlockSpec(memory_space=pl.ANY)] * (3 * len(held) + 3),
        out_specs=[pl.BlockSpec(memory_space=pl.ANY)] * 3,
        scratch_shapes=scratch,
        compiler_params=pltpu.CompilerParams(vmem_limit_bytes=limit),
    )(
        *offers,
        *weights,
        small,
    )
    return tuple(jnp.transpose(x, (1, 0, 2)) for x in outs)


def solution(mesh):
    in_specs = (
        P("rep", None, "dom"),
        P("rep", None, "dom"),
        P("rep", None, "dom"),
        P("rep", "dom"),
        P("rep", "dom"),
        P("rep", "dom", None),
        P("rep", "dom"),
    ) + (P(),) * 10
    out_specs = (P("rep", None, "dom"), P("rep", None, "dom"), P("rep", None, "dom"))
    step = functools.partial(local, mesh.shape["dom"], mesh.shape["rep"])
    return jax.shard_map(step, mesh=mesh, in_specs=in_specs, out_specs=out_specs, check_vma=False)
```

```python
import functools
import math

import jax
import jax.numpy as jnp
from jax import lax
from jax.experimental import pallas as pl
from jax.experimental.pallas import tpu as pltpu
from jax.sharding import PartitionSpec as P

NB = 8
TILE = 128
NEI = 4

slab_width = 1.5
time_step = 0.5
basis_width = 0.3
norm_eps = 1e-06

f32 = jnp.float32
bf16 = jnp.bfloat16

LOG2E = math.log2(math.e)
SCALE = math.sqrt(LOG2E) / basis_width
TOP = 34.0
UNLIFT = 2.0**-TOP
STEEP = 4.0 * LOG2E
FAR = (40.0 * LOG2E) ** 2


def distinct(offsets, count):
    return list(dict.fromkeys(o % count for o in offsets))


def domain_sets(count):
    layer1 = distinct([0, -1, 1], count)
    layer0 = distinct(layer1 + [o + s for o in layer1 for s in (-1, 1)], count)
    held = distinct(layer0 + [o + s for o in layer0 for s in (-1, 1)], count)
    return layer1, layer0, held


def dot(a, b):
    return jnp.dot(a, b, preferred_element_type=f32)


def pack_kernel(
    loc, speed, push, kinds, ghosts, lists, counts, inertia, swaps, levels, taper, out, small
):
    me = lax.axis_index("rep")
    lane = lax.broadcasted_iota(jnp.int32, (1, TILE), 1)
    factors, masses = jnp.zeros((1, TILE), f32), jnp.zeros((1, TILE), f32)
    for b in range(NB):
        scale = math.exp(-b * b) * UNLIFT / (math.sqrt(TILE * NEI * TILE) * SCALE)
        factors = jnp.where(lane == b, taper[b] * scale, factors)
    for s in range(inertia.shape[0]):
        masses = jnp.where(lane == s, inertia[s], masses)
    quotient = jnp.full((1, TILE), levels[me], f32) / jnp.full((1, TILE), levels[swaps[me]], f32)
    small[0:1] = factors
    small[1:2] = masses
    small[2:3] = jnp.sqrt(quotient)
    partner = swaps[me]
    rung = jnp.where(partner == me, 0, 1 + (jnp.minimum(me, partner) & 1))
    small[3:8] = jnp.full((5, TILE), rung, jnp.int32).astype(f32)
    labels = kinds[...]
    mass = jnp.zeros(labels.shape, f32)
    for s in range(inertia.shape[0]):
        mass = jnp.where(labels == s, inertia[s], mass)
    inv_mass = 1.0 / mass
    atoms, tiles = labels.shape[1], counts.shape[1]
    out[...] = jnp.zeros(out.shape, f32)
    for d in range(3):
        out[d : d + 1, 0:atoms] = (
            loc[d] + time_step * speed[d] + 0.5 * time_step * time_step * push[d] * inv_mass
        )
        out[3 + d : 4 + d, 0:atoms] = speed[d] + 0.5 * time_step * push[d] * inv_mass
    out[6:7, 0:atoms] = labels.astype(f32)
    out[7:8, 0 : ghosts.shape[1]] = ghosts[...].astype(f32)
    out[0:NEI, atoms : atoms + tiles] = lists[0].astype(f32)
    out[NEI : NEI + 1, atoms : atoms + tiles] = counts[...].astype(f32)


def weights_kernel(
    kind, coef, gain, mix, projections, wide, columns
):
    species = kind.shape[0]
    kinds_f = jnp.transpose(kind[...].astype(f32), (1, 0))
    coef_t = [jnp.transpose(coef[layer], (1, 0)) for layer in range(2)]
    u = []
    for b in range(NB):
        u.append(kinds_f * (coef_t[0][:, b : b + 1] * math.exp(-b * b)))
        columns[b] = jnp.broadcast_to(coef_t[1][:, b : b + 1] * math.exp(-b * b), columns.shape[1:])
    u = jnp.concatenate(u, axis=1)
    high = u.astype(bf16)
    wide[:, 0:TILE] = high
    wide[:, TILE : 2 * TILE] = (u - high.astype(f32)).astype(bf16)
    wide[:, 2 * TILE : 3 * TILE] = high
    gain_t = jnp.transpose(gain[...], (1, 0))
    for layer in range(2):
        columns[NB + layer] = jnp.broadcast_to(gain_t[:, layer : layer + 1], columns.shape[1:])
        wide[:, (3 + 2 * layer) * TILE : (4 + 2 * layer) * TILE] = jnp.transpose(
            mix[layer].astype(f32), (1, 0)
        ).astype(bf16)
    wide[:, 4 * TILE : 5 * TILE] = jnp.concatenate(
        [kinds_f, jnp.zeros((kinds_f.shape[0], TILE - species), f32)], axis=1
    ).astype(bf16)
    both = projections[...]
    high = both.astype(bf16)
    wide[:, 6 * TILE : 7 * TILE] = high
    wide[:, 7 * TILE : 8 * TILE] = (both - high.astype(f32)).astype(bf16)


def lanes_of(parts):
    return jnp.concatenate(parts, axis=1)


def activate(messages, gain):
    messages = messages * UNLIFT
    inverse = lax.rsqrt(jnp.mean(messages * messages, axis=0, keepdims=True) + norm_eps)
    v = messages * inverse * gain
    return (v / (1.0 + jnp.exp(-v))).astype(bf16)


def main_kernel(plan, *refs):
    count, atoms, ghost, species = plan
    layer1, layer0, held = domain_sets(count)
    tiles = atoms // TILE
    ghost_tiles = ghost // TILE
    ext_tiles = tiles + 2 * ghost_tiles
    n = len(held)
    offers = refs[: 3 * n]
    wide, columns, rung, small_in = refs[3 * n : 3 * n + 4]
    refs = refs[3 * n + 4 :]
    outputs = refs[:3]
    held_data, small, pos_out, vel_out, force_out, arrival, departures = refs[3:10]
    data = {o: held_data.at[at] for at, o in enumerate(held)}
    inward = pltpu.make_async_copy(small_in, small, arrival.at[0])
    inward.start()
    place = rung[3:4]
    for at in range(n):
        for first in range(0, atoms + TILE, TILE):
            lanes = slice(first, first + TILE)
            here, even, odd = (offers[3 * at + k][:, lanes] for k in range(3))
            held_data[at, :, lanes] = jnp.where(place == 0.0, here, jnp.where(place == 1.0, even, odd))

    (
        far_t,
        near_rhs,
        onehot,
        split_pos,
        species_sums,
        ghost_pick,
        hidden1,
        hidden2,
        ext_hidden,
        message_rows,
        envelopes,
        turned,
        asked,
        pulls,
        ints,
        sm,
        sem,
    ) = refs[10:-3]
    basis, squares = refs[-3], refs[-2:]
    u_parts = wide.at[:, 0 : 3 * TILE]
    mix_kind = wide.at[:, 3 * TILE : 4 * TILE + 16]
    mix_second = wide.at[:, 5 * TILE : 6 * TILE]
    both_parts = wide.at[:, 6 * TILE : 8 * TILE]
    kept = basis.shape[0]

    for at, o in enumerate(layer0):
        ints[at] = data[o][:, atoms : atoms + TILE].astype(jnp.int32)
    copies = [
        pltpu.make_async_copy(ints.at[at], sm.at[at], sem.at[at]) for at in range(len(layer0))
    ]
    for c in copies:
        c.start()

    outward = [
        pltpu.make_async_copy(src, dst, departures.at[at])
        for at, (src, dst) in enumerate(zip((pos_out, vel_out, force_out), outputs))
    ]
    for d in range(3):
        pos_out[d] = data[0][d : d + 1, 0:atoms]
    outward[0].start()

    row_id = lax.broadcasted_iota(jnp.int32, (8, TILE), 0)
    species_id = lax.broadcasted_iota(jnp.int32, (16, TILE), 0).astype(f32)
    def picked(o, first):
        src = data[o]
        idx = src[7:8, first : first + TILE].astype(jnp.int32)
        idx = jnp.broadcast_to(idx, (8, TILE))
        lane = idx & (TILE - 1)
        block = idx // TILE
        got = jnp.zeros((8, TILE), f32)
        for c in range(tiles):
            here = jnp.take_along_axis(
                src[:, c * TILE : (c + 1) * TILE], lane, axis=1, mode="promise_in_bounds"
            )
            got = jnp.where(block == c, here, got)
        return got

    def thirds(x):
        hi = x.astype(bf16).astype(f32)
        mid = (x - hi).astype(bf16).astype(f32)
        return hi, mid, x - hi - mid

    def rows_of(*rows):
        block = jnp.zeros((8, TILE), f32)
        for r, row in enumerate(rows):
            block = jnp.where(row_id == r, row, block)
        return block

    nowhere = rows_of(1e30, 0.0, 0.0, 1.0, 1.0, 1.0, 1.0)
    blank = jnp.zeros((8, TILE), f32)
    for at in range(len(layer0)):
        far_t[at, ext_tiles] = jnp.transpose(
            jnp.concatenate([blank] * 6 + [nowhere, rows_of(1e30)], axis=0), (1, 0)
        ).astype(bf16)

    for at, o in enumerate(layer0):
        lower, upper = (o - 1) % count, (o + 1) % count
        for e in range(ext_tiles):
            if e < tiles:
                block, shift = data[o][:, e * TILE : (e + 1) * TILE], 0.0
            elif e < tiles + ghost_tiles:
                block, shift = picked(lower, ghost + (e - tiles) * TILE), -slab_width
            else:
                block, shift = picked(upper, (e - tiles - ghost_tiles) * TILE), slab_width
            moved = jnp.where(row_id == 0, block + shift, block) - 0.5 * slab_width
            moved = jnp.where(row_id < 3, moved * SCALE, 0.0)
            onehot[at, e] = jnp.where(species_id == block[6:7, :], 1.0, 0.0).astype(bf16)
            hi, mid, low = thirds(moved)
            size = jnp.sum(moved * moved, axis=0, keepdims=True)
            sizes, steep_sizes = thirds(size), thirds(size * STEEP)
            far_t[at, e] = jnp.transpose(
                jnp.concatenate(
                    [hi, hi, hi, mid, mid, low]
                    + [rows_of(*sizes, 1.0, 1.0, 1.0, 1.0), rows_of(*steep_sizes)],
                    axis=0,
                ),
                (1, 0),
            ).astype(bf16)
            if o == 0:
                split_pos[e] = jnp.concatenate([hi, mid, low, rows_of(1.0)], axis=0).astype(bf16)
            if e < tiles:
                first, second, third = thirds(moved * -2.0)
                power = [-first, -second, -third, -first, -second, -first]
                power += [rows_of(-1.0, -1.0, -1.0, *[-x for x in sizes], TOP), blank]
                first, second, third = thirds(moved * (-2.0 * STEEP))
                steep = [first, second, third, first, second, first]
                steep += [rows_of(0.0, 0.0, 0.0, *steep_sizes), rows_of(1.0, 1.0, 1.0)]
                near_rhs[at, e] = lanes_of(
                    [jnp.concatenate(power, axis=0), jnp.concatenate(steep, axis=0)]
                ).astype(bf16)

    for c in copies:
        c.wait()

    def offsets(at, t):
        far = [
            far_t[at, jnp.where(k < sm[at, NEI, t], sm[at, k, t], ext_tiles)] for k in range(NEI)
        ]
        return dot(jnp.concatenate(far, axis=0), near_rhs[at, t])

    def basis_step(at, t, values):
        own = at == 0
        place = min(at, kept - 1)
        sums = [None] * (NB // 2)
        for half in range(NEI // 2):
            rows = slice(2 * half * TILE, 2 * (half + 1) * TILE)
            lhs = lanes_of([onehot[at, sm[at, 2 * half + k, t]] for k in range(2)])
            power = values[rows, 0:TILE]
            square = jnp.minimum(jnp.maximum(values[rows, TILE : 2 * TILE], 1e-30), FAR)
            slope = square * lax.rsqrt(square)
            ratio = jnp.exp2(slope)
            step = slope + slope
            envelope = None
            for p in range(NB // 2):
                even = jnp.exp2(power)
                odd = even * ratio
                pair = lanes_of([even.astype(bf16), odd.astype(bf16)])
                basis[place, t, rows, 2 * p * TILE : 2 * (p + 1) * TILE] = pair
                part = dot(lhs, pair)
                sums[p] = part if half == 0 else sums[p] + part
                if own:
                    part = even * small[0, 2 * p] + odd * small[0, 2 * p + 1]
                    envelope = part if p == 0 else envelope + part
                if p < NB // 2 - 1:
                    power = power + step
            if own:
                envelopes[t, rows] = envelope
        sums = [x[:, k * TILE : (k + 1) * TILE] for x in sums for k in range(2)]
        sums = jnp.concatenate(sums, axis=0)
        high = sums.astype(bf16)
        low = (sums - high.astype(f32)).astype(bf16)
        species_sums[at, t] = jnp.concatenate([high, high, low], axis=0)

    def first_layer(at):
        messages = dot(u_parts[...], lanes_of([species_sums[at, t] for t in range(tiles)]))
        activations = [
            activate(messages[:, t * TILE : (t + 1) * TILE], columns[NB]) for t in range(tiles)
        ]
        kinds = lanes_of([onehot[at, t] for t in range(tiles)])
        hidden = dot(mix_kind[...], jnp.concatenate([lanes_of(activations), kinds], axis=0))
        for t in range(tiles):
            block = hidden[:, t * TILE : (t + 1) * TILE].astype(bf16)
            hidden1[at, t] = block
            if at < len(layer1):
                ext_hidden[at, t] = block

    def pick_step(at, c):
        chosen = data[layer0[at]][7:8, 0 : 2 * ghost]
        rows = lax.broadcasted_iota(jnp.int32, (TILE, 2 * ghost), 0) + c * TILE
        ghost_pick[at, c * TILE : (c + 1) * TILE, :] = jnp.where(
            rows.astype(f32) == chosen, 1.0, 0.0
        ).astype(bf16)

    def extend(target, source_hidden, sets, o):
        for side, other in ((0, (o - 1) % count), (1, (o + 1) % count)):
            at = sets.index(other)
            rows = lanes_of([source_hidden[at, t] for t in range(tiles)])
            first = ghost if side == 0 else 0
            got = dot(
                rows, ghost_pick[layer0.index(other), :, first : first + ghost]
            ).astype(bf16)
            for g in range(ghost_tiles):
                target[tiles + side * ghost_tiles + g] = got[:, g * TILE : (g + 1) * TILE]

    def second_step(keep, t):
        at = layer0.index(layer1[keep])
        lhs = lanes_of([ext_hidden[keep, sm[at, k, t]] for k in range(NEI)])
        sums = dot(lhs, basis[keep, t])
        messages = None
        for b in range(NB):
            part = sums[:, b * TILE : (b + 1) * TILE] * columns[b]
            messages = part if messages is None else messages + part
        message_rows[keep, t] = messages

    def finish_second(keep, activations):
        at = layer0.index(layer1[keep])
        added = dot(mix_second[...], lanes_of(activations))
        for t in range(tiles):
            block = hidden1[at, t].astype(f32) + added[:, t * TILE : (t + 1) * TILE]
            hidden2[keep, t] = block.astype(bf16)

    def turn(block):
        return jnp.transpose(block.astype(f32), (1, 0)).astype(bf16)

    def import_final():
        extend(last, hidden2, layer1, 0)
        for e in range(tiles, ext_tiles):
            turned[e] = turn(last[e])

    last = ext_hidden.at[len(layer1)]
    order = list(range(1, len(layer1))) + [0]
    jobs = [
        functools.partial(pick_step, at, c) for at in range(len(layer0)) for c in range(tiles)
    ]
    imports = {
        keep: functools.partial(extend, ext_hidden.at[keep], hidden1, layer0, o)
        for keep, o in enumerate(layer1)
    }
    import_of = dict(imports)
    ready = set()

    def close_first(at):
        first_layer(at)
        ready.add(layer0[at])
        for keep, o in enumerate(layer1):
            if keep in imports and {(o - 1) % count, (o + 1) % count} <= ready:
                jobs.append(imports.pop(keep))

    inward.wait()
    sequence = [(at, t) for at in range(len(layer0)) for t in range(tiles)]
    squares[0][...] = offsets(0, 0)
    for i, (at, t) in enumerate(sequence):
        if i + 1 < len(sequence):
            upcoming = offsets(*sequence[i + 1])
        basis_step(at, t, squares[i % 2])
        if i + 1 < len(sequence):
            squares[(i + 1) % 2][...] = upcoming
        if at:
            for _ in range(min(len(jobs), 4)):
                jobs.pop(0)()
        if t == tiles - 1 and at < len(layer0) - 1:
            jobs.insert(0, functools.partial(close_first, at))
    for job in jobs:
        job()
    jobs = []
    close_first(len(layer0) - 1)
    if import_of[order[0]] in jobs:
        jobs.remove(import_of[order[0]])
        import_of[order[0]]()
    pending = list(jobs)

    for keep in order:
        activations = []
        for t in range(tiles):
            second_step(keep, t)
            if t:
                activations.append(activate(message_rows[keep, t - 1], columns[NB + 1]))
            if pending and t % 2:
                pending.pop(0)()
        activations.append(activate(message_rows[keep, tiles - 1], columns[NB + 1]))
        for job in pending:
            job()
        pending = [functools.partial(finish_second, keep, activations)]
        if keep and keep == order[-2]:
            pending.append(import_final)
    for job in pending:
        job()
    if len(order) == 1:
        import_final()
    own_hidden = [hidden2[0, t] for t in range(tiles)]
    for t in range(tiles):
        turned[t] = turn(own_hidden[t])
    own_hidden = lanes_of(own_hidden)
    wanted = dot(both_parts[...], jnp.concatenate([own_hidden, own_hidden], axis=0)).astype(bf16)
    empty = jnp.zeros((TILE, TILE), bf16)
    duos = range(tiles // 2)
    for q in duos:
        first, second = (wanted[:, t * TILE : (t + 1) * TILE] for t in (2 * q, 2 * q + 1))
        asked[q] = jnp.concatenate([lanes_of([first, empty]), lanes_of([empty, second])], axis=0)

    def weigh(q):
        lhs = [lanes_of([turned[sm[0, k, t]] for t in (2 * q, 2 * q + 1)]) for k in range(NEI)]
        scores = dot(jnp.concatenate(lhs, axis=0), asked[q])
        return (scores * lanes_of([envelopes[t] for t in (2 * q, 2 * q + 1)])).astype(bf16)

    def pull(q, weight):
        places = [
            lanes_of([split_pos[sm[0, k, t]] for k in range(NEI)]) for t in (2 * q, 2 * q + 1)
        ]
        got = dot(jnp.concatenate(places, axis=0), weight)
        for side in range(2):
            part = got[32 * side : 32 * (side + 1), side * TILE : (side + 1) * TILE]
            pulls[2 * q + side] = jnp.concatenate(
                [part[0:8] + part[8:16] + part[16:24], part[24:32]], axis=0
            )

    weights = {0: weigh(0)}
    for q in duos:
        if q + 1 in duos:
            weights[q + 1] = weigh(q + 1)
        pull(q, weights.pop(q))

    own = data[0]
    labels = own[6:7, 0:atoms]
    mass = jnp.zeros(labels.shape, f32)
    for s in range(species):
        mass = jnp.where(labels == s, small[1, s], mass)
    inv_mass = 1.0 / mass
    for t in range(tiles):
        lanes = slice(t * TILE, (t + 1) * TILE)
        got = pulls[t]
        force = got[0:8] - (own[:, lanes] - 0.5 * slab_width) * SCALE * got[8:9]
        velocity = own[3:6, lanes] + 0.5 * time_step * force[0:3] * inv_mass[:, lanes]
        velocity = velocity * small[2, 0]
        for d in range(3):
            force_out[d, :, lanes] = force[d : d + 1]
            vel_out[d, :, lanes] = velocity[d : d + 1]
    for c in outward[1:]:
        c.start()
    for c in outward:
        c.wait()


def local(
    count,
    replicas,
    particle_locations,
    particle_speeds,
    current_pushes,
    particle_kinds,
    halo_particle_labels,
    adjacent_block_labels,
    adjacent_place_totals,
    kind_vectors,
    kind_inertia,
    stepwise_distance_coefficients,
    signal_scaling_factors,
    feature_blend_coefficients,
    target_projection_array,
    source_projection_array,
    push_distance_taper,
    thermal_levels,
    granted_swaps,
):
    atoms = particle_locations.shape[2]
    ghost = halo_particle_labels.shape[1] // 2
    channels = kind_vectors.shape[1]
    tiles = atoms // TILE
    ext_tiles = tiles + 2 * (ghost // TILE)
    layer1, layer0, held = domain_sets(count)
    vmem = pl.BlockSpec(memory_space=pltpu.VMEM)
    smem = pl.BlockSpec(memory_space=pltpu.SMEM)
    shape = jax.ShapeDtypeStruct

    packed, small = pl.pallas_call(
        pack_kernel,
        out_shape=[shape((8, atoms + TILE), f32), shape((8, TILE), f32)],
        in_specs=[vmem] * 7 + [smem] * 4,
        out_specs=[vmem] * 2,
    )(
        jnp.transpose(particle_locations, (1, 0, 2)),
        jnp.transpose(particle_speeds, (1, 0, 2)),
        jnp.transpose(current_pushes, (1, 0, 2)),
        particle_kinds,
        halo_particle_labels,
        jnp.transpose(adjacent_block_labels, (0, 2, 1)),
        adjacent_place_totals,
        kind_inertia,
        granted_swaps,
        thermal_levels,
        push_distance_taper,
    )

    even = [(i, i ^ 1) for i in range(replicas)]
    odd = [(i, ((i + 1) ^ 1) - 1) for i in range(1, replicas - 1)]
    rim = [
        (r * count + d, r * count + (d + 1) % count) for r in (0, replicas - 1) for d in range(count)
    ]
    offers = []
    for o in held:
        beside = [((d + o) % count, d) for d in range(count)]
        here = packed if o == 0 else lax.ppermute(packed, "dom", beside)
        across = [(a * count + c, b * count + d) for a, b in odd for c, d in beside]
        offers += [
            here,
            lax.ppermute(here, "rep", even),
            lax.ppermute(packed, ("rep", "dom"), across + rim),
        ]
    projections = dot(source_projection_array, target_projection_array.T)
    weights = pl.pallas_call(
        weights_kernel,
        out_shape=[
            shape((channels, 8 * TILE), bf16),
            shape((NB + 2, channels, TILE), f32),
        ],
        in_specs=[vmem] * 5,
        out_specs=[vmem] * 2,
        compiler_params=pltpu.CompilerParams(vmem_limit_bytes=8 * 2**20),
        cost_estimate=pl.CostEstimate(flops=10**6, bytes_accessed=10**6, transcendentals=0),
    )(
        kind_vectors,
        stepwise_distance_coefficients,
        signal_scaling_factors,
        feature_blend_coefficients,
        projections,
    )

    n0, n1 = len(layer0), len(layer1)
    kept = (n1 + (n0 > n1), tiles, NEI * TILE, NB * TILE)
    buffers = [
        ((n0, ext_tiles + 1, TILE, 64), bf16),
        ((n0, tiles, 64, 2 * TILE), bf16),
        ((n0, ext_tiles, 16, TILE), bf16),
        ((ext_tiles, 32, TILE), bf16),
        ((n0, tiles, 3 * NB * 16, TILE), bf16),
        ((n0, atoms, 2 * ghost), bf16),
        ((n0, tiles, TILE, TILE), bf16),
        ((n1, tiles, TILE, TILE), bf16),
        ((n1 + 1, ext_tiles, TILE, TILE), bf16),
        ((n1, tiles, TILE, TILE), f32),
        ((tiles, NEI * TILE, TILE), f32),
        ((ext_tiles, TILE, TILE), bf16),
        ((tiles // 2, 2 * TILE, 2 * TILE), bf16),
        ((tiles, 16, TILE), f32),
        ((n0, 8, TILE), jnp.int32),
    ]
    inner = [
        ((len(held), 8, atoms + TILE), f32),
    ]
    outgoing = [((3, 1, atoms), f32)] * 3
    outer = [(kept, bf16)] + [((NEI * TILE, 2 * TILE), f32)] * 2
    scratch = [pltpu.VMEM(*buffer) for buffer in inner] + [pltpu.SMEM((8, TILE), f32)]
    scratch += [pltpu.VMEM(*buffer) for buffer in outgoing]
    scratch += [pltpu.SemaphoreType.DMA((1,)), pltpu.SemaphoreType.DMA((3,))]
    scratch += [pltpu.VMEM(*buffer) for buffer in buffers] + [
        pltpu.SMEM((n0, 8, TILE), jnp.int32),
        pltpu.SemaphoreType.DMA((n0,)),
    ]
    scratch += [pltpu.VMEM(*buffer) for buffer in outer]
    limit = 11 * 2**20 + sum(
        math.prod(dims[:-1]) * max(dims[-1], TILE) * jnp.dtype(kind).itemsize
        for dims, kind in inner + outgoing + buffers + outer
    )

    outs = pl.pallas_call(
        functools.partial(main_kernel, (count, atoms, ghost, kind_vectors.shape[0])),
        out_shape=[shape((3, 1, atoms), f32)] * 3,
        in_specs=[vmem] * (3 * len(held) + 3) + [pl.BlockSpec(memory_space=pl.ANY)],
        out_specs=[pl.BlockSpec(memory_space=pl.ANY)] * 3,
        scratch_shapes=scratch,
        compiler_params=pltpu.CompilerParams(vmem_limit_bytes=limit),
    )(
        *offers,
        *weights,
        small,
        small,
    )
    return tuple(jnp.transpose(x, (1, 0, 2)) for x in outs)


def solution(mesh):
    in_specs = (
        P("rep", None, "dom"),
        P("rep", None, "dom"),
        P("rep", None, "dom"),
        P("rep", "dom"),
        P("rep", "dom"),
        P("rep", "dom", None),
        P("rep", "dom"),
    ) + (P(),) * 10
    out_specs = (P("rep", None, "dom"), P("rep", None, "dom"), P("rep", None, "dom"))
    step = functools.partial(local, mesh.shape["dom"], mesh.shape["rep"])
    return jax.shard_map(step, mesh=mesh, in_specs=in_specs, out_specs=out_specs, check_vma=False)
```
